256 devices in a mesh: group: 8 (over x_hi, y), layer: 32 (over z, x_lo, core).
Axes of the slice: x: 4 (x_hi: 2, x_lo: 2; x = x_hi * 2 + x_lo), y: 4, z: 8, core: 2. Of those that a mesh axis runs over, the one named last changes fastest.
Arguments:
- query_grads: bfloat16 [1024, 131072], P('group', 'layer'), may hold values from -6 to 6
- query_ids: int32 [1024], P('group'), may hold values from 0 to 1023, each once
- train_feats: bfloat16 [8192, 131072], P('group', 'layer'), may hold values from -6 to 6
- basis_out: float32 [32, 64, 64], P('layer'), may hold values from -0.75 to 0.75
- basis_in: float32 [32, 64, 64], P('layer'), may hold values from -0.75 to 0.75
- eigen_vals: float32 [32, 64, 64], P('layer'), may hold values from 0.2 to 5
Outputs:
- scores: float32 [1024, 8192], P('layer', 'group')
The draws below stay inside these ranges and needn't reach their ends.
Inputs may be any that keep to these rules, and one draw needn't show every extreme that they name: `query_ids`: each number of 0 to 1023 appears exactly once.
All inputs are finite; a program needn't handle non-finite values.
Results may differ from the reference program's by a relative error of at most 0.0029.
Values may be sent and summed in bfloat16 or wider, within the bound.
A program may use at most 64 MiB of HBM per device.

```python
import math
import jax
import jax.numpy as jnp
from jax import lax

PROJ = 64
LAYERS = 32
FEATURES = 131072
QUERIES = 1024
TRAIN = 8192


def shard_levels(stream_key, shape, shards, smallest, top_value):
    gain = 1.0
    for position, shards_of in shards:
        steps = jax.random.uniform(jax.random.fold_in(jax.random.fold_in(stream_key, 6), position), (shards_of,), jnp.float32, smallest / len(shards), top_value / len(shards))
        gain = gain * jnp.repeat(jnp.exp(steps), shape[position] // shards_of).reshape((-1,) + (1,) * (len(shape) - 1 - position))
    return gain


def centred(key, extent, scale, bound, cuts=(), held_as=jnp.bfloat16):
    entries = jax.random.normal(key, extent, jnp.float32) * scale
    if len(cuts) > 0:
        entries = shard_levels(key, extent, cuts, -0.22, 0.18) * entries
    return jnp.clip(entries, min=-bound, max=bound).astype(held_as)


def setup_inputs(seed: int = 0) -> dict:
    key_of = jax.random.split(jax.random.key(seed), 7)
    return {
        "query_grads": centred(key_of[0], (QUERIES, FEATURES), 1.0, 6.0, ((0, 8), (1, 32))),
        "query_ids": jax.random.permutation(key_of[1], QUERIES).astype(jnp.int32),
        "train_feats": centred(key_of[2], (TRAIN, FEATURES), 1.0, 6.0, ((0, 8), (1, 32))),
        "basis_out": centred(key_of[3], (LAYERS, PROJ, PROJ), PROJ ** -0.5, 0.75, ((0, 32),), jnp.float32),
        "basis_in": centred(key_of[4], (LAYERS, PROJ, PROJ), PROJ ** -0.5, 0.75, ((0, 32),), jnp.float32),
        "eigen_vals": jnp.clip(jnp.exp(math.log(5.0) - 3.218876 * jax.random.uniform(key_of[5], (LAYERS, PROJ, PROJ), jnp.float32) ** shard_levels(key_of[5], (LAYERS, PROJ, PROJ), ((0, 32),), -0.2, 0.2)), 0.2, 5.0),
    }


damping = 0.1

def precondition(grads, basis_out, basis_in, eigen_vals):
    width = basis_out.shape[-1]
    square = grads.reshape(grads.shape[0], width, width).astype(jnp.float32)
    rotated = jnp.einsum('ai,qab,bj->qij', basis_out, square, basis_in, precision=lax.Precision.HIGHEST)
    scaled = rotated / (eigen_vals + damping)
    restored = jnp.einsum('ai,qij,bj->qab', basis_out, scaled, basis_in, precision=lax.Precision.HIGHEST)
    return restored.reshape(grads.shape[0], width * width).astype(jnp.bfloat16)

def reference(query_grads, query_ids, train_feats, basis_out, basis_in, eigen_vals):
    width = PROJ * PROJ

    def layer_step(total, layer):
        start = (layer * width).astype(jnp.int32)
        queries = lax.dynamic_slice_in_dim(query_grads, start, width, 1)
        trains = lax.dynamic_slice_in_dim(train_feats, start, width, 1)
        out_basis = lax.dynamic_index_in_dim(basis_out, layer, 0, keepdims=False)
        in_basis = lax.dynamic_index_in_dim(basis_in, layer, 0, keepdims=False)
        values = lax.dynamic_index_in_dim(eigen_vals, layer, 0, keepdims=False)
        prepared = precondition(queries, out_basis, in_basis, values)
        term = jnp.einsum('qf,tf->qt', prepared.astype(jnp.float32), trains.astype(jnp.float32), preferred_element_type=jnp.float32)
        return (total + term, None)
    total, _ = lax.scan(layer_step, jnp.zeros((QUERIES, TRAIN), jnp.float32), jnp.arange(LAYERS, dtype=jnp.int32))
    scale = 1.0 / math.sqrt(FEATURES)
    return jnp.zeros((QUERIES, TRAIN), jnp.float32).at[query_ids].set(total * scale)
```

```python
import functools
import math

import jax
import jax.numpy as jnp
from jax import lax
from jax.experimental import pallas as pl
from jax.experimental.pallas import tpu as pltpu
from jax.sharding import PartitionSpec as P

damping = 0.1
MESH = pl.DeviceIdType.MESH
f32, bf16 = jnp.float32, jnp.bfloat16

SIZES = {"a": (512, 640, 512, 640), "b": (384, 512, 384, 512)}
PIECES = {}
row = 0
for part in "ab":
    for place, size in enumerate(SIZES[part]):
        PIECES[part + str(place)] = (row, row + size)
        row += size
PART = {"a": (0, 2304), "b": (2304, 4096)}
NAMES = list(PIECES)
UP = ("0", "1", "2", "3")
DOWN = ("2", "3", "0", "1")


def split(x):
    high = x.astype(bf16)
    return high, (x - high.astype(f32)).astype(bf16)


def diagonal(block):
    width = block.shape[0]
    four = jnp.concatenate([block] * 4, axis=1)
    four = jnp.concatenate([four] * 4, axis=0)
    rows = lax.broadcasted_iota(jnp.int32, four.shape, 0) // width
    cols = lax.broadcasted_iota(jnp.int32, four.shape, 1) // width
    return jnp.where(rows == cols, four, 0.0)


def apply_basis(matrix, x):
    high, low = split(x)
    both = jnp.dot(matrix, high, preferred_element_type=f32)
    rest = jnp.dot(matrix[:256], low, preferred_element_type=f32)
    return both[:256] + both[256:] + rest


def kernel(
    g_hbm, ids_ref, t_hbm, bo_ref, bi_ref, eig_ref, out_ref,
    g_v, t_v, q, y1, y2, inv, bdm, acc, cx, rs_send, rs_recv, sums, ids, hot, a_send, a_recv,
    load_sem, q_send, q_recv, id_send, id_recv, cx_ssem, cx_rsem, rs_ssem, rs_rsem, a_ssem, a_rsem,
):
    group, layer = lax.axis_index("group"), lax.axis_index("layer")
    xh, y = group // 4, group % 4
    me, core = layer // 2, layer % 2
    up = (xh * 4 + lax.rem(y + 1, 4), layer)
    down = (xh * 4 + lax.rem(y + 3, 4), layer)
    across = ((1 - xh) * 4 + y, layer)
    sibling = (group, me * 2 + 1 - core)

    barrier = pltpu.get_barrier_semaphore()

    def greet_group(k, c):
        pl.semaphore_signal(barrier, inc=1, device_id=(lax.rem(group + k, 8), layer), device_id_type=MESH)
        return c

    def greet_layer(k, c):
        pl.semaphore_signal(barrier, inc=1, device_id=(group, lax.rem(layer + k, 32)), device_id_type=MESH)
        return c

    lax.fori_loop(1, 8, greet_group, 0)
    lax.fori_loop(1, 32, greet_layer, 0)

    load_g = pltpu.make_async_copy(g_hbm, g_v, load_sem.at[0])
    load_t = pltpu.make_async_copy(t_hbm, t_v, load_sem.at[1])
    load_g.start()
    load_t.start()

    bo = diagonal(bo_ref[...])
    bi = diagonal(bi_ref[...])
    for place, matrix in enumerate((bi.T, bo.T, bo, bi)):
        high, low = split(matrix)
        bdm[place, 0:256, :] = high
        bdm[place, 256:512, :] = low
    scale = 1.0 / (eig_ref[...] + damping)
    for j in range(64):
        inv[j * 64 : j * 64 + 64, :] = jnp.broadcast_to(scale[:, j : j + 1], (64, 128))

    load_g.wait()

    def stage_a(u, c):
        base = pl.multiple_of(u * 512, 512)
        left = g_v[:, pl.ds(base, 256)]
        right = g_v[:, pl.ds(base + 256, 256)]
        both = lax.dot_general(
            bdm[0], jnp.concatenate([left, right], axis=0), (((1,), (1,)), ((), ())), preferred_element_type=f32
        )
        r = both[:256] + both[256:]
        y1[pl.ds(base, 256), :] = r[:, :128]
        y1[pl.ds(base + 256, 256), :] = r[:, 128:]
        return c

    def strided(ref, u):
        halves = []
        for h in range(2):
            halves.append(
                jnp.concatenate([ref[pl.ds(u * 8 + h * 4 + s, 64, stride=64), :] for s in range(4)], axis=0)
            )
        return jnp.concatenate(halves, axis=1)

    def stage_bc(u, c):
        base = pl.multiple_of(u * 512, 512)
        r = apply_basis(bdm[1], strided(y1, u))
        r = r * jnp.concatenate([inv[pl.ds(base, 256), :], inv[pl.ds(base + 256, 256), :]], axis=1)
        r = apply_basis(bdm[2], r)
        y2[pl.ds(base, 256), :] = r[:, :128]
        y2[pl.ds(base + 256, 256), :] = r[:, 128:]
        return c

    def stage_d(u, c):
        base = pl.multiple_of(u * 512, 512)
        r = apply_basis(bdm[3], strided(y2, u)).astype(bf16)
        q[0, pl.ds(base, 256), :] = r[:, :128]
        q[0, pl.ds(base + 256, 256), :] = r[:, 128:]
        return c

    lax.fori_loop(0, 8, stage_a, 0)
    lax.fori_loop(0, 8, stage_bc, 0)
    lax.fori_loop(0, 8, stage_d, 0)

    pl.semaphore_wait(barrier, 38)

    sends = []

    def send(src_slot, piece, target, dst_slot):
        lo, hi = PIECES[piece]
        copy = pltpu.make_async_remote_copy(
            src_ref=q.at[src_slot, pl.ds(lo, hi - lo)],
            dst_ref=q.at[dst_slot, pl.ds(lo, hi - lo)],
            send_sem=q_send.at[len(sends)],
            recv_sem=q_recv.at[dst_slot * 8 + NAMES.index(piece)],
            device_id=target,
            device_id_type=MESH,
        )
        copy.start()
        sends.append(copy)

    def arrive(slot, piece):
        lo, hi = PIECES[piece]
        part = q.at[slot, pl.ds(lo, hi - lo)]
        pltpu.make_async_remote_copy(
            src_ref=part, dst_ref=part, send_sem=q_send.at[0], recv_sem=q_recv.at[slot * 8 + NAMES.index(piece)],
            device_id=up, device_id_type=MESH,
        ).wait_recv()

    for n in "0123":
        send(0, "a" + n, across, 4)
    for above, below in zip(UP, DOWN):
        send(0, "b" + above, up, 3)
        send(0, "b" + below, down, 1)
    for n in "0123":
        send(0, "b" + n, across, 4)
    for above, below in zip(UP, DOWN):
        send(0, "a" + above, up, 3)
        send(0, "a" + below, down, 1)

    def id_target(k):
        return (lax.rem(xh + k // 4, 2) * 4 + lax.rem(y + k, 4), layer)

    def id_slot(k):
        return k // 4 * 4 + (4 - k % 4) % 4

    id_copies = []
    for k in range(1, 8):
        copy = pltpu.make_async_remote_copy(
            src_ref=ids_ref, dst_ref=ids.at[id_slot(k)], send_sem=id_send.at[id_slot(k)], recv_sem=id_recv.at[id_slot(k)],
            device_id=id_target(k), device_id_type=MESH,
        )
        copy.start()
        id_copies.append(copy)
    ids[0] = ids_ref[...]

    def multiply(slot, lo, hi, first):
        def tile(i, c):
            rows = pl.ds(pl.multiple_of(i * 512, 512), 512)
            r = jnp.dot(t_v[rows, lo:hi], q[slot, lo:hi, :], preferred_element_type=f32)
            acc[slot, rows, :] = r if first else acc[slot, rows, :] + r
            return c

        lax.fori_loop(0, 2, tile, 0)

    mine = pl.multiple_of(core * 512, 512)
    theirs = pl.multiple_of((1 - core) * 512, 512)

    def exchange(slot):
        return pltpu.make_async_remote_copy(
            src_ref=acc.at[slot, pl.ds(theirs, 512)], dst_ref=cx.at[slot], send_sem=cx_ssem.at[slot],
            recv_sem=cx_rsem.at[slot], device_id=sibling, device_id_type=MESH,
        )

    def scatter(slot):
        exchange(slot).wait_recv()
        rs_send[slot] = (acc[slot, pl.ds(mine, 512), :] + cx[slot]).astype(bf16)

        def one(k, c):
            to = lax.rem(me + k, 16)
            pltpu.make_async_remote_copy(
                src_ref=rs_send.at[slot, pl.ds(pl.multiple_of(to * 32, 32), 32)],
                dst_ref=rs_recv.at[slot, pl.ds(pl.multiple_of((k - 1) * 32, 32), 32)],
                send_sem=rs_ssem.at[slot], recv_sem=rs_rsem.at[slot],
                device_id=(group, to * 2 + core), device_id_type=MESH,
            ).start()
            return c

        lax.fori_loop(1, 16, one, 0)

    def scattered(slot):
        return pltpu.make_async_remote_copy(
            src_ref=rs_recv.at[slot], dst_ref=rs_recv.at[slot], send_sem=rs_ssem.at[slot], recv_sem=rs_rsem.at[slot],
            device_id=up, device_id_type=MESH,
        )

    def collect(slot):
        scattered(slot).wait_recv()
        own = pl.multiple_of(me * 32, 32)
        total = acc[slot, pl.ds(mine + own, 32), :] + cx[slot, pl.ds(own, 32), :]
        for k in range(15):
            total = total + rs_recv[slot, k * 32 : k * 32 + 32, :].astype(f32)
        sums[:, slot * 128 : slot * 128 + 128] = total

    a, b = PART["a"], PART["b"]
    load_t.wait()
    multiply(0, 0, 4096, True)
    exchange(0).start()

    for n, above, below in zip("0123", UP, DOWN):
        arrive(4, "a" + n)
        send(4, "a" + n, up, 7)
        send(4, "a" + n, down, 5)
        arrive(3, "b" + above)
        if above in "01":
            send(3, "b" + above, up, 2)
        send(3, "b" + above, across, 7)
        arrive(1, "b" + below)
        if below in "23":
            send(1, "b" + below, down, 2)
        send(1, "b" + below, across, 5)
        if n == "0":
            scatter(0)
    multiply(4, *a, True)
    multiply(3, *b, True)
    multiply(1, *b, True)
    for n in "0213":
        arrive(2, "b" + n)
        send(2, "b" + n, across, 6)
    multiply(2, *b, True)
    collect(0)
    for n in "0123":
        arrive(4, "b" + n)
    multiply(4, *b, False)
    exchange(4).start()
    for above, below in zip(UP, DOWN):
        arrive(3, "a" + above)
        if above in "01":
            send(3, "a" + above, up, 2)
        arrive(1, "a" + below)
        if below in "23":
            send(1, "a" + below, down, 2)
    multiply(3, *a, False)
    exchange(3).start()
    multiply(1, *a, False)
    exchange(1).start()
    scatter(4)

    for copy in id_copies:
        copy.wait_recv()
    rows = lax.broadcasted_iota(jnp.int32, (256, 128), 0)
    rows = rows // 8 * 32 + rows % 8
    for k in range(4):
        for s in range(8):
            same = rows + 8 * k == ids[s]
            hot[k * 256 : k * 256 + 256, s * 128 : s * 128 + 128] = jnp.where(same, 1.0, 0.0).astype(bf16)

    scatter(3)
    scatter(1)
    for above, below in zip(UP, DOWN):
        arrive(7, "a" + above)
        if above in "01":
            send(7, "a" + above, up, 6)
        arrive(5, "a" + below)
        if below in "23":
            send(5, "a" + below, down, 6)
    for n in "0213":
        arrive(2, "a" + n)
    multiply(2, *a, False)
    exchange(2).start()
    multiply(7, *a, True)
    multiply(5, *a, True)
    scatter(2)
    collect(4)
    collect(3)
    collect(1)
    for above, below in zip(UP, DOWN):
        arrive(7, "b" + above)
        arrive(5, "b" + below)
    multiply(7, *b, False)
    exchange(7).start()
    multiply(5, *b, False)
    exchange(5).start()
    scatter(7)
    scatter(5)
    collect(2)
    for n in "0213":
        arrive(6, "a" + n)
    multiply(6, *a, True)
    for n in "0213":
        arrive(6, "b" + n)
    multiply(6, *b, False)
    exchange(6).start()
    collect(7)
    collect(5)
    scatter(6)
    collect(6)

    high, low = split(sums[...])
    placed = lax.dot_general(
        hot[...], jnp.concatenate([high, low], axis=0), (((1,), (1,)), ((), ())), preferred_element_type=f32
    )
    placed = (placed[:, :32] + placed[:, 32:]) * (1.0 / math.sqrt(131072))
    placed = jnp.concatenate([placed[k * 256 : k * 256 + 256] for k in range(4)], axis=1)
    a_send[...] = placed.reshape(32, 8, 128)

    place = core * 16 + me

    def deal(k, c):
        to = lax.rem(layer + k, 32)
        pltpu.make_async_remote_copy(
            src_ref=a_send.at[to], dst_ref=a_recv.at[place], send_sem=a_ssem.at[0], recv_sem=a_rsem.at[0],
            device_id=(group, to), device_id_type=MESH,
        ).start()
        return c

    lax.fori_loop(1, 32, deal, 0)
    a_recv[place] = a_send[layer]
    dealt = pltpu.make_async_remote_copy(
        src_ref=a_recv.at[pl.ds(0, 31)], dst_ref=a_recv.at[pl.ds(0, 31)], send_sem=a_ssem.at[0], recv_sem=a_rsem.at[0],
        device_id=up, device_id_type=MESH,
    )
    dealt.wait_recv()
    for m in range(8):
        tiles = [a_recv[4 * m + n] for n in range(4)]
        for k in range(4):
            out_ref[8 * k : 8 * k + 8, 128 * m : 128 * m + 128] = jnp.concatenate(
                [tile[:, 32 * k : 32 * k + 32] for tile in tiles], axis=1
            )

    for copy in sends:
        copy.wait_send()
    for copy in id_copies:
        copy.wait_send()
    for slot in range(8):
        exchange(slot).wait_send()
        scattered(slot).wait_send()
    dealt.wait_send()


def on_device(query_grads, query_ids, train_feats, basis_out, basis_in, eigen_vals):
    anywhere = pl.BlockSpec(memory_space=pl.ANY)
    vmem = pl.BlockSpec(memory_space=pltpu.VMEM)
    dma = pltpu.SemaphoreType.DMA
    return pl.pallas_call(
        kernel,
        out_shape=jax.ShapeDtypeStruct((32, 1024), f32),
        in_specs=[anywhere, vmem, anywhere, vmem, vmem, vmem],
        out_specs=vmem,
        scratch_shapes=[
            pltpu.VMEM((128, 4096), bf16),
            pltpu.VMEM((1024, 4096), bf16),
            pltpu.VMEM((8, 4096, 128), bf16),
            pltpu.VMEM((4096, 128), f32),
            pltpu.VMEM((4096, 128), f32),
            pltpu.VMEM((4096, 128), f32),
            pltpu.VMEM((4, 512, 256), bf16),
            pltpu.VMEM((8, 1024, 128), f32),
            pltpu.VMEM((8, 512, 128), f32),
            pltpu.VMEM((8, 512, 128), bf16),
            pltpu.VMEM((8, 480, 128), bf16),
            pltpu.VMEM((32, 1024), f32),
            pltpu.VMEM((8, 1, 128), jnp.int32),
            pltpu.VMEM((1024, 1024), bf16),
            pltpu.VMEM((32, 8, 128), f32),
            pltpu.VMEM((32, 8, 128), f32),
            dma((2,)),
            dma((56,)),
            dma((64,)),
            dma((8,)),
            dma((8,)),
            dma((8,)),
            dma((8,)),
            dma((8,)),
            dma((8,)),
            dma((1,)),
            dma((1,)),
        ],
        compiler_params=pltpu.CompilerParams(
            collective_id=0, has_side_effects=True, vmem_limit_bytes=56 * 2**20
        ),
        name="influence",
    )(
        query_grads,
        query_ids.reshape(1, 128),
        train_feats,
        basis_out[0],
        basis_in[0],
        eigen_vals[0],
    )


def solution(mesh):
    return jax.shard_map(
        on_device,
        mesh=mesh,
        in_specs=(
            P("group", "layer"),
            P("group"),
            P("group", "layer"),
            P("layer", None, None),
            P("layer", None, None),
            P("layer", None, None),
        ),
        out_specs=P("layer", "group"),
        check_vma=False,
    )
```

```python
import functools
import math

import jax
import jax.numpy as jnp
from jax import lax
from jax.experimental import pallas as pl
from jax.experimental.pallas import tpu as pltpu
from jax.sharding import PartitionSpec as P

damping = 0.1
MESH = pl.DeviceIdType.MESH
f32, bf16 = jnp.float32, jnp.bfloat16

SIZES = {"a": (512, 640, 512, 640), "b": (384, 512, 384, 512)}
PIECES = {}
row = 0
for part in "ab":
    for place, size in enumerate(SIZES[part]):
        PIECES[part + str(place)] = (row, row + size)
        row += size
PART = {"a": (0, 2304), "b": (2304, 4096)}
NAMES = list(PIECES)
UP = ("0", "1", "2", "3")
LAST = 6
DOWN = ("2", "3", "0", "1")


def split(x):
    high = x.astype(bf16)
    return high, (x - high.astype(f32)).astype(bf16)


def diagonal(block):
    width = block.shape[0]
    four = jnp.concatenate([block] * 4, axis=1)
    four = jnp.concatenate([four] * 4, axis=0)
    rows = lax.broadcasted_iota(jnp.int32, four.shape, 0) // width
    cols = lax.broadcasted_iota(jnp.int32, four.shape, 1) // width
    return jnp.where(rows == cols, four, 0.0)


def far(n, count):
    return count // 2 + (n % 2 * 2 - 1) * ((n + 1) // 2)


def apply_basis(matrix, x):
    high, low = split(x)
    both = jnp.dot(matrix, high, preferred_element_type=f32)
    rest = jnp.dot(matrix[:256], low, preferred_element_type=f32)
    return both[:256] + both[256:] + rest


def kernel(
    g_hbm, ids_ref, t_hbm, bo_ref, bi_ref, eig_ref, out_ref,
    g_v, t_v, q, y1, y2, inv, bdm, acc, cx, rs_send, rs_recv, zs, xs, ids, hot, a_send, a_recv,
    load_sem, q_send, q_recv, id_send, id_recv, cx_ssem, cx_rsem, rs_ssem, rs_rsem, xs_ssem, xs_rsem, a_ssem, a_rsem,
):
    group, layer = lax.axis_index("group"), lax.axis_index("layer")
    xh, y = group // 4, group % 4
    me, core = layer // 2, layer % 2
    z, xl = me // 2, me % 2
    up = (xh * 4 + lax.rem(y + 1, 4), layer)
    down = (xh * 4 + lax.rem(y + 3, 4), layer)
    across = ((1 - xh) * 4 + y, layer)
    sibling = (group, me * 2 + 1 - core)

    barrier = pltpu.get_barrier_semaphore()

    def greet_group(k, c):
        pl.semaphore_signal(barrier, inc=1, device_id=(lax.rem(group + k, 8), layer), device_id_type=MESH)
        return c

    def greet_layer(k, c):
        pl.semaphore_signal(barrier, inc=1, device_id=(group, lax.rem(layer + k, 32)), device_id_type=MESH)
        return c

    lax.fori_loop(1, 8, greet_group, 0)
    lax.fori_loop(1, 32, greet_layer, 0)

    load_g = pltpu.make_async_copy(g_hbm, g_v, load_sem.at[0])
    load_t = pltpu.make_async_copy(t_hbm, t_v, load_sem.at[1])
    load_g.start()
    load_t.start()

    bo = diagonal(bo_ref[...])
    bi = diagonal(bi_ref[...])
    for place, matrix in enumerate((bi.T, bo.T, bo, bi)):
        high, low = split(matrix)
        bdm[place, 0:256, :] = high
        bdm[place, 256:512, :] = low
    scale = 1.0 / (eig_ref[...] + damping)
    for j in range(64):
        inv[j * 64 : j * 64 + 64, :] = jnp.broadcast_to(scale[:, j : j + 1], (64, 128))

    load_g.wait()

    def stage_a(u, c):
        base = pl.multiple_of(u * 512, 512)
        left = g_v[:, pl.ds(base, 256)]
        right = g_v[:, pl.ds(base + 256, 256)]
        both = lax.dot_general(
            bdm[0], jnp.concatenate([left, right], axis=0), (((1,), (1,)), ((), ())), preferred_element_type=f32
        )
        r = both[:256] + both[256:]
        y1[pl.ds(base, 256), :] = r[:, :128]
        y1[pl.ds(base + 256, 256), :] = r[:, 128:]
        return c

    def strided(ref, u):
        halves = []
        for h in range(2):
            halves.append(
                jnp.concatenate([ref[pl.ds(u * 8 + h * 4 + s, 64, stride=64), :] for s in range(4)], axis=0)
            )
        return jnp.concatenate(halves, axis=1)

    def stage_bc(u, c):
        base = pl.multiple_of(u * 512, 512)
        r = apply_basis(bdm[1], strided(y1, u))
        r = r * jnp.concatenate([inv[pl.ds(base, 256), :], inv[pl.ds(base + 256, 256), :]], axis=1)
        r = apply_basis(bdm[2], r)
        y2[pl.ds(base, 256), :] = r[:, :128]
        y2[pl.ds(base + 256, 256), :] = r[:, 128:]
        return c

    def stage_d(u, c):
        base = pl.multiple_of(u * 512, 512)
        r = apply_basis(bdm[3], strided(y2, u)).astype(bf16)
        q[0, pl.ds(base, 256), :] = r[:, :128]
        q[0, pl.ds(base + 256, 256), :] = r[:, 128:]
        return c

    lax.fori_loop(0, 8, stage_a, 0, unroll=8)
    lax.fori_loop(0, 8, stage_bc, 0, unroll=8)
    lax.fori_loop(0, 8, stage_d, 0, unroll=8)

    pl.semaphore_wait(barrier, 38)

    sends = []

    def send(src_slot, piece, target, dst_slot):
        lo, hi = PIECES[piece]
        copy = pltpu.make_async_remote_copy(
            src_ref=q.at[src_slot, pl.ds(lo, hi - lo)],
            dst_ref=q.at[dst_slot, pl.ds(lo, hi - lo)],
            send_sem=q_send.at[len(sends)],
            recv_sem=q_recv.at[dst_slot * 8 + NAMES.index(piece)],
            device_id=target,
            device_id_type=MESH,
        )
        copy.start()
        sends.append(copy)

    def arrive(slot, piece):
        lo, hi = PIECES[piece]
        part = q.at[slot, pl.ds(lo, hi - lo)]
        pltpu.make_async_remote_copy(
            src_ref=part, dst_ref=part, send_sem=q_send.at[0], recv_sem=q_recv.at[slot * 8 + NAMES.index(piece)],
            device_id=up, device_id_type=MESH,
        ).wait_recv()

    for n in "0123":
        send(0, "a" + n, across, 4)
    for above, below in zip(UP, DOWN):
        send(0, "b" + above, up, 3)
        send(0, "b" + below, down, 1)
    for n in "0123":
        send(0, "b" + n, across, 4)

    def id_target(k):
        return (lax.rem(xh + k // 4, 2) * 4 + lax.rem(y + k, 4), layer)

    def id_slot(k):
        return k // 4 * 4 + (4 - k % 4) % 4

    id_copies = []
    for k in range(1, 8):
        copy = pltpu.make_async_remote_copy(
            src_ref=ids_ref, dst_ref=ids.at[id_slot(k)], send_sem=id_send.at[id_slot(k)], recv_sem=id_recv.at[id_slot(k)],
            device_id=id_target(k), device_id_type=MESH,
        )
        copy.start()
        id_copies.append(copy)
    ids[0] = ids_ref[...]

    def multiply(slot, lo, hi, first):
        def tile(i, c):
            rows = pl.ds(pl.multiple_of(i * 512, 512), 512)
            r = jnp.dot(t_v[rows, lo:hi], q[slot, lo:hi, :], preferred_element_type=f32)
            acc[slot, rows, :] = r if first else acc[slot, rows, :] + r
            return c

        lax.fori_loop(0, 2, tile, 0)

    mine = pl.multiple_of(core * 512, 512)
    theirs = pl.multiple_of((1 - core) * 512, 512)

    def exchange(slot):
        return pltpu.make_async_remote_copy(
            src_ref=acc.at[slot, pl.ds(theirs, 512)], dst_ref=cx.at[slot], send_sem=cx_ssem.at[slot],
            recv_sem=cx_rsem.at[slot], device_id=sibling, device_id_type=MESH,
        )

    def scatter(slot):
        exchange(slot).wait_recv()
        rs_send[slot] = (acc[slot, pl.ds(mine, 512), :] + cx[slot]).astype(bf16)
        count, size = (16, 32) if slot == LAST else (8, 64)
        here = me if slot == LAST else z

        def one(n, c):
            k = far(n, count)
            to = lax.rem(here + k, count)
            target = to * 2 + core if slot == LAST else to * 4 + xl * 2 + core
            pltpu.make_async_remote_copy(
                src_ref=rs_send.at[slot, pl.ds(pl.multiple_of(to * size, size), size)],
                dst_ref=rs_recv.at[slot, pl.ds(pl.multiple_of((k - 1) * size, size), size)],
                send_sem=rs_ssem.at[slot], recv_sem=rs_rsem.at[slot],
                device_id=(group, target), device_id_type=MESH,
            ).start()
            return c

        lax.fori_loop(0, count - 1, one, 0)

    def scattered(slot):
        landed = rs_recv.at[slot, pl.ds(0, 480 if slot == LAST else 448)]
        return pltpu.make_async_remote_copy(
            src_ref=landed, dst_ref=landed, send_sem=rs_ssem.at[slot], recv_sem=rs_rsem.at[slot],
            device_id=up, device_id_type=MESH,
        )

    def summed(slot, size):
        scattered(slot).wait_recv()
        own = pl.multiple_of((me if slot == LAST else z) * size, size)
        total = acc[slot, pl.ds(mine + own, size), :] + cx[slot, pl.ds(own, size), :]
        for k in range(512 // size - 1):
            total = total + rs_recv[slot, k * size : k * size + size, :].astype(f32)
        return total

    def swap(slot):
        return pltpu.make_async_remote_copy(
            src_ref=zs.at[slot, pl.ds(pl.multiple_of((1 - xl) * 32, 32), 32)], dst_ref=xs.at[slot],
            send_sem=xs_ssem.at[slot], recv_sem=xs_rsem.at[slot],
            device_id=(group, z * 4 + (1 - xl) * 2 + core), device_id_type=MESH,
        )

    def zsum(slot):
        zs[slot] = summed(slot, 64)
        swap(slot).start()

    def collect(slot):
        if slot == LAST:
            total = summed(slot, 32)
        else:
            swap(slot).wait_recv()
            total = zs[slot, pl.ds(pl.multiple_of(xl * 32, 32), 32), :] + xs[slot]
        placed = None
        for half in split(total):
            none = jnp.zeros_like(half)
            spread = jnp.concatenate(
                [jnp.concatenate([half if m == k else none for m in range(4)], axis=1) for k in range(4)], axis=0
            )
            term = lax.dot_general(hot[slot], spread, (((1,), (1,)), ((), ())), preferred_element_type=f32)
            placed = term if placed is None else placed + term
        placed = placed.reshape(32, 8, 128)
        a_send[...] = placed if slot == 0 else a_send[...] + placed

    def piece(slot, name, first):
        arrive(slot, name)
        multiply(slot, *PIECES[name], first)

    a, b = PART["a"], PART["b"]
    load_t.wait()
    multiply(0, 0, 4096, True)
    exchange(0).start()

    def neighbours_b(above, below):
        arrive(3, "b" + above)
        arrive(1, "b" + below)
        if above in "01":
            send(3, "b" + above, up, 2)
            send(1, "b" + below, down, 2)
        send(3, "b" + above, across, 7)
        send(1, "b" + below, across, 5)

    def partner_a(n):
        arrive(4, "a" + n)
        send(4, "a" + n, up, 7)
        send(4, "a" + n, down, 5)

    def neighbours_a(above, below):
        arrive(3, "a" + above)
        arrive(1, "a" + below)
        if above in "01":
            send(3, "a" + above, up, 2)
            send(1, "a" + below, down, 2)

    def second_a(above, below):
        arrive(7, "a" + above)
        arrive(5, "a" + below)
        if above in "01":
            send(7, "a" + above, up, 6)
            send(5, "a" + below, down, 6)

    neighbours_b("0", "2")
    neighbours_b("1", "3")
    for above, below in zip(UP, DOWN):
        send(0, "a" + above, up, 3)
        send(0, "a" + below, down, 1)
    partner_a("0")
    scatter(0)
    partner_a("1")
    neighbours_b("2", "0")
    neighbours_b("3", "1")
    partner_a("2")

    for copy in id_copies:
        copy.wait_recv()
    rows = lax.broadcasted_iota(jnp.int32, (256, 128), 0)
    rows = rows // 8 * 32 + rows % 8
    for s in range(8):
        for k in range(4):
            same = rows + 8 * k == ids[s]
            hot[s, :, k * 128 : k * 128 + 128] = jnp.where(same, 1.0, 0.0).astype(bf16)

    partner_a("3")
    multiply(4, *a, True)
    for n in "0213":
        arrive(2, "b" + n)
        send(2, "b" + n, across, 6)
    multiply(3, *b, True)
    multiply(1, *b, True)
    neighbours_a("0", "2")
    multiply(2, *b, True)
    neighbours_a("1", "3")
    for n in "0123":
        arrive(4, "b" + n)
    multiply(4, *b, False)
    exchange(4).start()
    zsum(0)
    neighbours_a("2", "0")
    scatter(4)
    neighbours_a("3", "1")
    multiply(3, *a, False)
    exchange(3).start()
    multiply(1, *a, False)
    exchange(1).start()
    second_a("0", "2")
    scatter(3)
    second_a("1", "3")
    scatter(1)
    zsum(4)
    second_a("2", "0")
    second_a("3", "1")
    multiply(7, *a, True)
    multiply(5, *a, True)
    zsum(3)
    for n in "0123":
        arrive(7, "b" + n)
    multiply(7, *b, False)
    exchange(7).start()
    for n in "0123":
        arrive(5, "b" + n)
    multiply(5, *b, False)
    exchange(5).start()
    zsum(1)
    for n in "0213":
        arrive(2, "a" + n)
    scatter(7)
    multiply(2, *a, False)
    exchange(2).start()
    scatter(5)
    collect(0)
    piece(6, "b0", True)
    piece(6, "b2", False)
    scatter(2)
    piece(6, "a0", False)
    piece(6, "a2", False)
    piece(6, "b1", False)
    zsum(7)
    piece(6, "b3", False)
    piece(6, "a1", False)
    piece(6, "a3", False)
    exchange(6).start()
    zsum(5)
    collect(4)
    scatter(6)
    zsum(2)
    collect(3)
    collect(1)
    collect(7)
    collect(5)
    collect(2)
    collect(6)

    place = core * 16 + me

    def deal(n, c):
        to = lax.rem(layer + far(n, 32), 32)
        pltpu.make_async_remote_copy(
            src_ref=a_send.at[to], dst_ref=a_recv.at[place], send_sem=a_ssem.at[0], recv_sem=a_rsem.at[0],
            device_id=(group, to), device_id_type=MESH,
        ).start()
        return c

    lax.fori_loop(0, 31, deal, 0)
    a_recv[place] = a_send[layer]
    dealt = pltpu.make_async_remote_copy(
        src_ref=a_recv.at[pl.ds(0, 31)], dst_ref=a_recv.at[pl.ds(0, 31)], send_sem=a_ssem.at[0], recv_sem=a_rsem.at[0],
        device_id=up, device_id_type=MESH,
    )
    dealt.wait_recv()
    for m in range(8):
        tiles = [a_recv[4 * m + n] for n in range(4)]
        for k in range(4):
            out_ref[8 * k : 8 * k + 8, 128 * m : 128 * m + 128] = jnp.concatenate(
                [tile[:, 32 * k : 32 * k + 32] for tile in tiles], axis=1
            )

    for copy in sends:
        copy.wait_send()
    for copy in id_copies:
        copy.wait_send()
    for slot in range(8):
        exchange(slot).wait_send()
        scattered(slot).wait_send()
        if slot != LAST:
            swap(slot).wait_send()
    dealt.wait_send()


def on_device(query_grads, query_ids, train_feats, basis_out, basis_in, eigen_vals):
    anywhere = pl.BlockSpec(memory_space=pl.ANY)
    vmem = pl.BlockSpec(memory_space=pltpu.VMEM)
    dma = pltpu.SemaphoreType.DMA
    return pl.pallas_call(
        kernel,
        out_shape=jax.ShapeDtypeStruct((32, 1024), f32),
        in_specs=[anywhere, vmem, anywhere, vmem, vmem, vmem],
        out_specs=vmem,
        scratch_shapes=[
            pltpu.VMEM((128, 4096), bf16),
            pltpu.VMEM((1024, 4096), bf16),
            pltpu.VMEM((8, 4096, 128), bf16),
            pltpu.VMEM((4096, 128), f32),
            pltpu.VMEM((4096, 128), f32),
            pltpu.VMEM((4096, 128), f32),
            pltpu.VMEM((4, 512, 256), bf16),
            pltpu.VMEM((8, 1024, 128), f32),
            pltpu.VMEM((8, 512, 128), f32),
            pltpu.VMEM((8, 512, 128), bf16),
            pltpu.VMEM((8, 480, 128), bf16),
            pltpu.VMEM((8, 64, 128), f32),
            pltpu.VMEM((8, 32, 128), f32),
            pltpu.VMEM((8, 1, 128), jnp.int32),
            pltpu.VMEM((8, 256, 512), bf16),
            pltpu.VMEM((32, 8, 128), f32),
            pltpu.VMEM((32, 8, 128), f32),
            dma((2,)),
            dma((56,)),
            dma((64,)),
            dma((8,)),
            dma((8,)),
            dma((8,)),
            dma((8,)),
            dma((8,)),
            dma((8,)),
            dma((8,)),
            dma((8,)),
            dma((1,)),
            dma((1,)),
        ],
        compiler_params=pltpu.CompilerParams(
            collective_id=0, has_side_effects=True, vmem_limit_bytes=56 * 2**20
        ),
        name="influence",
    )(
        query_grads,
        query_ids.reshape(1, 128),
        train_feats,
        basis_out[0],
        basis_in[0],
        eigen_vals[0],
    ) * (1.0 / math.sqrt(131072))


def solution(mesh):
    return jax.shard_map(
        on_device,
        mesh=mesh,
        in_specs=(
            P("group", "layer"),
            P("group"),
            P("group", "layer"),
            P("layer", None, None),
            P("layer", None, None),
            P("layer", None, None),
        ),
        out_specs=P("layer", "group"),
        check_vma=False,
    )
```

```python
import functools
import math

import jax
import jax.numpy as jnp
from jax import lax
from jax.experimental import pallas as pl
from jax.experimental.pallas import tpu as pltpu
from jax.sharding import PartitionSpec as P

damping = 0.1
MESH = pl.DeviceIdType.MESH
f32, bf16 = jnp.float32, jnp.bfloat16

ORDER = (
    ("a0", 512), ("b0", 384), ("b2", 384), ("a1", 640), ("a2", 512), ("b1", 512), ("b3", 512), ("a3", 640),
)
PIECES = {}
row = 0
for name, size in ORDER:
    PIECES[name] = (row, row + size)
    row += size
NAMES = list(PIECES)
A = ((0, 512), (1280, 2432), (3456, 4096))
B = ((512, 1280), (2432, 3456))
UP = ("0", "1", "2", "3")
LAST = 6
DOWN = ("2", "3", "0", "1")


def split(x):
    high = x.astype(bf16)
    return high, (x - high.astype(f32)).astype(bf16)


def diagonal(block):
    width = block.shape[0]
    four = jnp.concatenate([block] * 4, axis=1)
    four = jnp.concatenate([four] * 4, axis=0)
    rows = lax.broadcasted_iota(jnp.int32, four.shape, 0) // width
    cols = lax.broadcasted_iota(jnp.int32, four.shape, 1) // width
    return jnp.where(rows == cols, four, 0.0)


def far(n, count):
    return count // 2 + (n % 2 * 2 - 1) * ((n + 1) // 2)


def apply_basis(matrix, x):
    high, low = split(x)
    both = jnp.dot(matrix, high, preferred_element_type=f32)
    rest = jnp.dot(matrix[:256], low, preferred_element_type=f32)
    return both[:256] + both[256:] + rest


def kernel(
    g_hbm, ids_ref, t_hbm, bo_ref, bi_ref, eig_ref, out_ref,
    g_v, t_v, q, y1, y2, inv, bdm, acc, cx, rs_send, rs_recv, zs, xs, ids, hot, a_send, a_recv,
    load_sem, q_send, q_recv, id_send, id_recv, cx_ssem, cx_rsem, rs_ssem, rs_rsem, xs_ssem, xs_rsem, a_ssem, a_rsem,
):
    group, layer = lax.axis_index("group"), lax.axis_index("layer")
    xh, y = group // 4, group % 4
    me, core = layer // 2, layer % 2
    z, xl = me // 2, me % 2
    up = (xh * 4 + lax.rem(y + 1, 4), layer)
    down = (xh * 4 + lax.rem(y + 3, 4), layer)
    across = ((1 - xh) * 4 + y, layer)
    sibling = (group, me * 2 + 1 - core)

    load_g = pltpu.make_async_copy(g_hbm, g_v, load_sem.at[0])
    load_t = pltpu.make_async_copy(t_hbm, t_v, load_sem.at[1])
    load_g.start()

    barrier = pltpu.get_barrier_semaphore()

    def greet_group(k, c):
        pl.semaphore_signal(barrier, inc=1, device_id=(lax.rem(group + k, 8), layer), device_id_type=MESH)
        return c

    def greet_layer(k, c):
        pl.semaphore_signal(barrier, inc=1, device_id=(group, lax.rem(layer + k, 32)), device_id_type=MESH)
        return c

    lax.fori_loop(1, 8, greet_group, 0, unroll=7)
    lax.fori_loop(1, 32, greet_layer, 0, unroll=31)
    load_t.start()

    bo = diagonal(bo_ref[...])
    bi = diagonal(bi_ref[...])
    for place, matrix in enumerate((bi.T, bo.T, bo, bi)):
        high, low = split(matrix)
        bdm[place, 0:256, :] = high
        bdm[place, 256:512, :] = low
    scale = 1.0 / (eig_ref[...] + damping)
    for j in range(64):
        inv[j * 64 : j * 64 + 64, :] = jnp.broadcast_to(scale[:, j : j + 1], (64, 128))

    load_g.wait()

    def stage_a(u, c):
        base = pl.multiple_of(u * 512, 512)
        left = g_v[:, pl.ds(base, 256)]
        right = g_v[:, pl.ds(base + 256, 256)]
        both = lax.dot_general(
            bdm[0], jnp.concatenate([left, right], axis=0), (((1,), (1,)), ((), ())), preferred_element_type=f32
        )
        r = both[:256] + both[256:]
        y1[pl.ds(base, 256), :] = r[:, :128]
        y1[pl.ds(base + 256, 256), :] = r[:, 128:]
        return c

    def strided(ref, u):
        halves = []
        for h in range(2):
            halves.append(
                jnp.concatenate([ref[pl.ds(u * 8 + h * 4 + s, 64, stride=64), :] for s in range(4)], axis=0)
            )
        return jnp.concatenate(halves, axis=1)

    def stage_bc(u, c):
        base = pl.multiple_of(u * 512, 512)
        r = apply_basis(bdm[1], strided(y1, u))
        r = r * jnp.concatenate([inv[pl.ds(base, 256), :], inv[pl.ds(base + 256, 256), :]], axis=1)
        r = apply_basis(bdm[2], r)
        y2[pl.ds(base, 256), :] = r[:, :128]
        y2[pl.ds(base + 256, 256), :] = r[:, 128:]
        return c

    def stage_d(u, c):
        base = pl.multiple_of(u * 512, 512)
        r = apply_basis(bdm[3], strided(y2, u)).astype(bf16)
        q[0, pl.ds(base, 256), :] = r[:, :128]
        q[0, pl.ds(base + 256, 256), :] = r[:, 128:]
        return c

    lax.fori_loop(0, 8, stage_a, 0, unroll=8)
    lax.fori_loop(0, 8, stage_bc, 0, unroll=8)
    lax.fori_loop(0, 3, stage_d, 0, unroll=3)

    pl.semaphore_wait(barrier, 38)

    sends = []

    def send(src_slot, piece, target, dst_slot):
        lo, hi = PIECES[piece]
        copy = pltpu.make_async_remote_copy(
            src_ref=q.at[src_slot, pl.ds(lo, hi - lo)],
            dst_ref=q.at[dst_slot, pl.ds(lo, hi - lo)],
            send_sem=q_send.at[len(sends)],
            recv_sem=q_recv.at[dst_slot * 8 + NAMES.index(piece)],
            device_id=target,
            device_id_type=MESH,
        )
        copy.start()
        sends.append(copy)

    def arrive(slot, piece):
        lo, hi = PIECES[piece]
        part = q.at[slot, pl.ds(lo, hi - lo)]
        pltpu.make_async_remote_copy(
            src_ref=part, dst_ref=part, send_sem=q_send.at[0], recv_sem=q_recv.at[slot * 8 + NAMES.index(piece)],
            device_id=up, device_id_type=MESH,
        ).wait_recv()

    send(0, "a0", across, 4)
    send(0, "b0", up, 3)
    send(0, "b2", down, 1)
    lax.fori_loop(3, 8, stage_d, 0, unroll=5)
    for n in "123":
        send(0, "a" + n, across, 4)
    for above, below in zip(UP[1:], DOWN[1:]):
        send(0, "b" + above, up, 3)
        send(0, "b" + below, down, 1)
    for n in "0123":
        send(0, "b" + n, across, 4)

    def id_target(k):
        return (lax.rem(xh + k // 4, 2) * 4 + lax.rem(y + k, 4), layer)

    def id_slot(k):
        return k // 4 * 4 + (4 - k % 4) % 4

    id_copies = []
    for k in range(1, 8):
        copy = pltpu.make_async_remote_copy(
            src_ref=ids_ref, dst_ref=ids.at[id_slot(k)], send_sem=id_send.at[id_slot(k)], recv_sem=id_recv.at[id_slot(k)],
            device_id=id_target(k), device_id_type=MESH,
        )
        copy.start()
        id_copies.append(copy)
    ids[0] = ids_ref[...]

    mine = pl.multiple_of(core * 512, 512)
    theirs = pl.multiple_of((1 - core) * 512, 512)

    def half(slot, ranges, first, start):
        r = None if first else acc[slot, pl.ds(start, 512), :]
        for lo, hi in ranges:
            term = jnp.dot(t_v[pl.ds(start, 512), lo:hi], q[slot, lo:hi, :], preferred_element_type=f32)
            r = term if r is None else r + term
        acc[slot, pl.ds(start, 512), :] = r

    def multiply(slot, ranges, first):
        def tile(i, c):
            half(slot, ranges, first, pl.multiple_of(i * 512, 512))
            return c

        lax.fori_loop(0, 2, tile, 0)

    def exchange(slot):
        return pltpu.make_async_remote_copy(
            src_ref=acc.at[slot, pl.ds(theirs, 512)], dst_ref=cx.at[slot], send_sem=cx_ssem.at[slot],
            recv_sem=cx_rsem.at[slot], device_id=sibling, device_id_type=MESH,
        )

    def scatter(slot):
        exchange(slot).wait_recv()
        rs_send[slot] = (acc[slot, pl.ds(mine, 512), :] + cx[slot]).astype(bf16)
        count, size = (16, 32) if slot == LAST else (8, 64)
        here = me if slot == LAST else z

        def one(n, c):
            k = far(n, count)
            to = lax.rem(here + k, count)
            target = to * 2 + core if slot == LAST else to * 4 + xl * 2 + core
            pltpu.make_async_remote_copy(
                src_ref=rs_send.at[slot, pl.ds(pl.multiple_of(to * size, size), size)],
                dst_ref=rs_recv.at[slot, pl.ds(pl.multiple_of((k - 1) * size, size), size)],
                send_sem=rs_ssem.at[slot], recv_sem=rs_rsem.at[slot],
                device_id=(group, target), device_id_type=MESH,
            ).start()
            return c

        lax.fori_loop(0, count - 1, one, 0, unroll=count - 1)

    def scattered(slot):
        landed = rs_recv.at[slot, pl.ds(0, 480 if slot == LAST else 448)]
        return pltpu.make_async_remote_copy(
            src_ref=landed, dst_ref=landed, send_sem=rs_ssem.at[slot], recv_sem=rs_rsem.at[slot],
            device_id=up, device_id_type=MESH,
        )

    def summed(slot, size):
        scattered(slot).wait_recv()
        own = pl.multiple_of((me if slot == LAST else z) * size, size)
        total = acc[slot, pl.ds(mine + own, size), :] + cx[slot, pl.ds(own, size), :]
        for k in range(512 // size - 1):
            total = total + rs_recv[slot, k * size : k * size + size, :].astype(f32)
        return total

    def swap(slot):
        return pltpu.make_async_remote_copy(
            src_ref=zs.at[slot, pl.ds(pl.multiple_of((1 - xl) * 32, 32), 32)], dst_ref=xs.at[slot],
            send_sem=xs_ssem.at[slot], recv_sem=xs_rsem.at[slot],
            device_id=(group, z * 4 + (1 - xl) * 2 + core), device_id_type=MESH,
        )

    def zsum(slot):
        zs[slot] = summed(slot, 64)

    def collect(slot):
        if slot == LAST:
            total = summed(slot, 32)
        else:
            swap(slot).wait_recv()
            total = zs[slot, pl.ds(pl.multiple_of(xl * 32, 32), 32), :] + xs[slot]
        placed = None
        for half in split(total):
            none = jnp.zeros_like(half)
            spread = jnp.concatenate(
                [jnp.concatenate([half if m == k else none for m in range(4)], axis=1) for k in range(4)], axis=0
            )
            term = lax.dot_general(hot[slot], spread, (((1,), (1,)), ((), ())), preferred_element_type=f32)
            placed = term if placed is None else placed + term
        placed = placed.reshape(32, 8, 128)
        a_send[...] = placed if slot == 0 else a_send[...] + placed

    def piece(slot, name, first):
        arrive(slot, name)
        multiply(slot, (PIECES[name],), first)

    load_t.wait()
    multiply(0, ((0, 4096),), True)
    exchange(0).start()

    def neighbours_b(above, below):
        arrive(3, "b" + above)
        arrive(1, "b" + below)
        if above in "01":
            send(3, "b" + above, up, 2)
            send(1, "b" + below, down, 2)
        send(3, "b" + above, across, 7)
        send(1, "b" + below, across, 5)

    def partner_a(n):
        arrive(4, "a" + n)
        send(4, "a" + n, up, 7)
        send(4, "a" + n, down, 5)

    def neighbours_a(above, below):
        arrive(3, "a" + above)
        arrive(1, "a" + below)
        if above in "01":
            send(3, "a" + above, up, 2)
            send(1, "a" + below, down, 2)

    def second_a(above, below):
        arrive(7, "a" + above)
        arrive(5, "a" + below)
        if above in "01":
            send(7, "a" + above, up, 6)
            send(5, "a" + below, down, 6)

    neighbours_b("0", "2")
    neighbours_b("1", "3")
    for above, below in zip(UP, DOWN):
        send(0, "a" + above, up, 3)
        send(0, "a" + below, down, 1)
    partner_a("0")
    scatter(0)
    partner_a("1")
    neighbours_b("2", "0")
    neighbours_b("3", "1")
    partner_a("2")

    for copy in id_copies:
        copy.wait_recv()
    rows = lax.broadcasted_iota(jnp.int32, (256, 128), 0)
    rows = rows // 8 * 32 + rows % 8
    for s in range(8):
        for k in range(4):
            same = rows + 8 * k == ids[s]
            hot[s, :, k * 128 : k * 128 + 128] = jnp.where(same, 1.0, 0.0).astype(bf16)

    partner_a("3")
    multiply(4, A, True)
    for n in "0213":
        arrive(2, "b" + n)
        send(2, "b" + n, across, 6)
    multiply(3, B, True)
    multiply(1, B, True)
    neighbours_a("0", "2")
    multiply(2, B, True)
    neighbours_a("1", "3")
    for n in "0123":
        arrive(4, "b" + n)
    multiply(4, B, False)
    exchange(4).start()
    zsum(0)
    neighbours_a("2", "0")
    scatter(4)
    neighbours_a("3", "1")
    multiply(3, A, False)
    exchange(3).start()
    multiply(1, A, False)
    exchange(1).start()
    second_a("0", "2")
    scatter(3)
    second_a("1", "3")
    scatter(1)
    zsum(4)
    second_a("2", "0")
    second_a("3", "1")
    multiply(7, A, True)
    multiply(5, A, True)
    zsum(3)
    for n in "0123":
        arrive(7, "b" + n)
    multiply(7, B, False)
    exchange(7).start()
    for n in "0123":
        arrive(5, "b" + n)
    multiply(5, B, False)
    exchange(5).start()
    zsum(1)
    for n in "0213":
        arrive(2, "a" + n)
    scatter(7)
    multiply(2, A, False)
    exchange(2).start()
    scatter(5)
    for slot in (0, 4, 3, 1):
        swap(slot).start()
    piece(6, "b0", True)
    piece(6, "b2", False)
    scatter(2)
    piece(6, "a0", False)
    piece(6, "a2", False)
    piece(6, "b1", False)
    piece(6, "b3", False)
    piece(6, "a1", False)
    arrive(6, "a3")
    half(6, (PIECES["a3"],), False, theirs)
    exchange(6).start()
    half(6, (PIECES["a3"],), False, mine)
    zsum(7)
    swap(7).start()
    collect(0)
    scatter(6)
    zsum(5)
    swap(5).start()
    zsum(2)
    swap(2).start()
    collect(4)
    collect(3)
    collect(1)
    collect(7)
    collect(5)
    collect(2)
    collect(6)

    place = core * 16 + me

    def deal(n, c):
        to = lax.rem(layer + far(n, 32), 32)
        pltpu.make_async_remote_copy(
            src_ref=a_send.at[to], dst_ref=a_recv.at[place], send_sem=a_ssem.at[0], recv_sem=a_rsem.at[0],
            device_id=(group, to), device_id_type=MESH,
        ).start()
        return c

    lax.fori_loop(0, 31, deal, 0, unroll=31)
    a_recv[place] = a_send[layer]
    dealt = pltpu.make_async_remote_copy(
        src_ref=a_recv.at[pl.ds(0, 31)], dst_ref=a_recv.at[pl.ds(0, 31)], send_sem=a_ssem.at[0], recv_sem=a_rsem.at[0],
        device_id=up, device_id_type=MESH,
    )
    dealt.wait_recv()
    for m in range(8):
        tiles = [a_recv[4 * m + n] for n in range(4)]
        for k in range(4):
            out_ref[8 * k : 8 * k + 8, 128 * m : 128 * m + 128] = jnp.concatenate(
                [tile[:, 32 * k : 32 * k + 32] for tile in tiles], axis=1
            )

    for copy in sends:
        copy.wait_send()
    for copy in id_copies:
        copy.wait_send()
    for slot in range(8):
        exchange(slot).wait_send()
        scattered(slot).wait_send()
        if slot != LAST:
            swap(slot).wait_send()
    dealt.wait_send()


def on_device(query_grads, query_ids, train_feats, basis_out, basis_in, eigen_vals):
    anywhere = pl.BlockSpec(memory_space=pl.ANY)
    vmem = pl.BlockSpec(memory_space=pltpu.VMEM)
    dma = pltpu.SemaphoreType.DMA
    return pl.pallas_call(
        kernel,
        out_shape=jax.ShapeDtypeStruct((32, 1024), f32),
        in_specs=[anywhere, vmem, anywhere, vmem, vmem, vmem],
        out_specs=vmem,
        scratch_shapes=[
            pltpu.VMEM((128, 4096), bf16),
            pltpu.VMEM((1024, 4096), bf16),
            pltpu.VMEM((8, 4096, 128), bf16),
            pltpu.VMEM((4096, 128), f32),
            pltpu.VMEM((4096, 128), f32),
            pltpu.VMEM((4096, 128), f32),
            pltpu.VMEM((4, 512, 256), bf16),
            pltpu.VMEM((8, 1024, 128), f32),
            pltpu.VMEM((8, 512, 128), f32),
            pltpu.VMEM((8, 512, 128), bf16),
            pltpu.VMEM((8, 480, 128), bf16),
            pltpu.VMEM((8, 64, 128), f32),
            pltpu.VMEM((8, 32, 128), f32),
            pltpu.VMEM((8, 1, 128), jnp.int32),
            pltpu.VMEM((8, 256, 512), bf16),
            pltpu.VMEM((32, 8, 128), f32),
            pltpu.VMEM((32, 8, 128), f32),
            dma((2,)),
            dma((56,)),
            dma((64,)),
            dma((8,)),
            dma((8,)),
            dma((8,)),
            dma((8,)),
            dma((8,)),
            dma((8,)),
            dma((8,)),
            dma((8,)),
            dma((1,)),
            dma((1,)),
        ],
        compiler_params=pltpu.CompilerParams(
            collective_id=0, has_side_effects=True, vmem_limit_bytes=56 * 2**20
        ),
        name="influence",
    )(
        query_grads,
        query_ids.reshape(1, 128),
        train_feats,
        basis_out[0],
        basis_in[0],
        eigen_vals[0],
    ) * (1.0 / math.sqrt(131072))


def solution(mesh):
    return jax.shard_map(
        on_device,
        mesh=mesh,
        in_specs=(
            P("group", "layer"),
            P("group"),
            P("group", "layer"),
            P("layer", None, None),
            P("layer", None, None),
            P("layer", None, None),
        ),
        out_specs=P("layer", "group"),
        check_vma=False,
    )
```

```python
import functools
import math

import jax
import jax.numpy as jnp
from jax import lax
from jax.experimental import pallas as pl
from jax.experimental.pallas import tpu as pltpu
from jax.sharding import PartitionSpec as P

damping = 0.1
MESH = pl.DeviceIdType.MESH
f32, bf16 = jnp.float32, jnp.bfloat16

ORDER = (
    ("a0", 512), ("b0", 384), ("b2", 384), ("a1", 640), ("a2", 512), ("b1", 512), ("b3", 512), ("a3", 640),
)
PIECES = {}
row = 0
for name, size in ORDER:
    PIECES[name] = (row, row + size)
    row += size
NAMES = list(PIECES)
A = ((0, 512), (1280, 2432), (3456, 4096))
B = ((512, 1280), (2432, 3456))
UP = ("0", "1", "2", "3")
LAST = 6
PITCH = 72
DOWN = ("2", "3", "0", "1")


def split(x):
    high = x.astype(bf16)
    return high, (x - high.astype(f32)).astype(bf16)


def diagonal(block):
    width = block.shape[0]
    four = jnp.concatenate([block] * 4, axis=1)
    four = jnp.concatenate([four] * 4, axis=0)
    rows = lax.broadcasted_iota(jnp.int32, four.shape, 0) // width
    cols = lax.broadcasted_iota(jnp.int32, four.shape, 1) // width
    return jnp.where(rows == cols, four, 0.0)


def far(n, count):
    return count // 2 + (n % 2 * 2 - 1) * ((n + 1) // 2)


def apply_basis(matrix, x):
    high, low = split(x)
    both = jnp.dot(matrix, high, preferred_element_type=f32)
    rest = jnp.dot(matrix[:256], low, preferred_element_type=f32)
    return both[:256] + both[256:] + rest


def kernel(
    g_hbm, ids_ref, t_hbm, bo_ref, bi_ref, eig_ref, out_ref,
    g_v, t_v, q, y1, y2, inv, bdm, acc, cx, rs_send, rs_recv, zs, xs, ids, hot, a_send, a_recv,
    load_sem, q_send, q_recv, id_send, id_recv, cx_ssem, cx_rsem, rs_ssem, rs_rsem, xs_ssem, xs_rsem, a_ssem, a_rsem,
):
    group, layer = lax.axis_index("group"), lax.axis_index("layer")
    xh, y = group // 4, group % 4
    me, core = layer // 2, layer % 2
    z, xl = me // 2, me % 2
    up = (xh * 4 + lax.rem(y + 1, 4), layer)
    down = (xh * 4 + lax.rem(y + 3, 4), layer)
    across = ((1 - xh) * 4 + y, layer)
    sibling = (group, me * 2 + 1 - core)

    load_g = pltpu.make_async_copy(g_hbm, g_v, load_sem.at[0])
    load_t = pltpu.make_async_copy(t_hbm, t_v, load_sem.at[1])
    load_g.start()

    barrier = pltpu.get_barrier_semaphore()

    def greet_group(k, c):
        pl.semaphore_signal(barrier, inc=1, device_id=(lax.rem(group + k, 8), layer), device_id_type=MESH)
        return c

    def greet_layer(k, c):
        pl.semaphore_signal(barrier, inc=1, device_id=(group, lax.rem(layer + k, 32)), device_id_type=MESH)
        return c

    lax.fori_loop(1, 8, greet_group, 0, unroll=7)
    lax.fori_loop(1, 32, greet_layer, 0, unroll=31)
    load_t.start()

    bo = diagonal(bo_ref[...])
    bi = diagonal(bi_ref[...])
    for place, matrix in enumerate((bi.T, bo.T, bo, bi)):
        high, low = split(matrix)
        bdm[place, 0:256, :] = high
        bdm[place, 256:512, :] = low
    scale = 1.0 / (eig_ref[...] + damping)
    for j in range(64):
        inv[j * 64 : j * 64 + 64, :] = jnp.broadcast_to(scale[:, j : j + 1], (64, 128))

    load_g.wait()

    def spread(ref, u, r):
        for h in range(2):
            for s in range(4):
                start = pl.multiple_of((u * 8 + h * 4 + s) * PITCH, 8)
                ref[pl.ds(start, 64), :] = r[s * 64 : s * 64 + 64, h * 128 : h * 128 + 128]

    def stage_a(u, c):
        base = pl.multiple_of(u * 512, 512)
        left = g_v[:, pl.ds(base, 256)]
        right = g_v[:, pl.ds(base + 256, 256)]
        both = lax.dot_general(
            bdm[0], jnp.concatenate([left, right], axis=0), (((1,), (1,)), ((), ())), preferred_element_type=f32
        )
        r = both[:256] + both[256:]
        spread(y1, u, r)
        return c

    def strided(ref, u):
        halves = []
        for h in range(2):
            halves.append(
                jnp.concatenate([ref[pl.ds(u * 8 + h * 4 + s, 64, stride=PITCH), :] for s in range(4)], axis=0)
            )
        return jnp.concatenate(halves, axis=1)

    def stage_bc(u, c):
        base = pl.multiple_of(u * 512, 512)
        r = apply_basis(bdm[1], strided(y1, u))
        r = r * jnp.concatenate([inv[pl.ds(base, 256), :], inv[pl.ds(base + 256, 256), :]], axis=1)
        r = apply_basis(bdm[2], r)
        spread(y2, u, r)
        return c

    def stage_d(u, c):
        base = pl.multiple_of(u * 512, 512)
        r = apply_basis(bdm[3], strided(y2, u)).astype(bf16)
        q[0, pl.ds(base, 256), :] = r[:, :128]
        q[0, pl.ds(base + 256, 256), :] = r[:, 128:]
        return c

    lax.fori_loop(0, 8, stage_a, 0, unroll=8)
    lax.fori_loop(0, 8, stage_bc, 0, unroll=8)
    lax.fori_loop(0, 3, stage_d, 0, unroll=3)

    pl.semaphore_wait(barrier, 38)

    sends = []

    def send(src_slot, piece, target, dst_slot):
        lo, hi = PIECES[piece]
        copy = pltpu.make_async_remote_copy(
            src_ref=q.at[src_slot, pl.ds(lo, hi - lo)],
            dst_ref=q.at[dst_slot, pl.ds(lo, hi - lo)],
            send_sem=q_send.at[len(sends)],
            recv_sem=q_recv.at[dst_slot * 8 + NAMES.index(piece)],
            device_id=target,
            device_id_type=MESH,
        )
        copy.start()
        sends.append(copy)

    def arrive(slot, piece):
        lo, hi = PIECES[piece]
        part = q.at[slot, pl.ds(lo, hi - lo)]
        pltpu.make_async_remote_copy(
            src_ref=part, dst_ref=part, send_sem=q_send.at[0], recv_sem=q_recv.at[slot * 8 + NAMES.index(piece)],
            device_id=up, device_id_type=MESH,
        ).wait_recv()

    send(0, "a0", across, 4)
    send(0, "b0", up, 3)
    send(0, "b2", down, 1)
    lax.fori_loop(3, 8, stage_d, 0, unroll=5)
    for n in "123":
        send(0, "a" + n, across, 4)
    for above, below in zip(UP[1:], DOWN[1:]):
        send(0, "b" + above, up, 3)
        send(0, "b" + below, down, 1)
    for n in "0123":
        send(0, "b" + n, across, 4)

    def id_target(k):
        return (lax.rem(xh + k // 4, 2) * 4 + lax.rem(y + k, 4), layer)

    def id_slot(k):
        return k // 4 * 4 + (4 - k % 4) % 4

    id_copies = []
    for k in range(1, 8):
        copy = pltpu.make_async_remote_copy(
            src_ref=ids_ref, dst_ref=ids.at[id_slot(k)], send_sem=id_send.at[id_slot(k)], recv_sem=id_recv.at[id_slot(k)],
            device_id=id_target(k), device_id_type=MESH,
        )
        copy.start()
        id_copies.append(copy)
    ids[0] = ids_ref[...]

    mine = pl.multiple_of(core * 512, 512)
    theirs = pl.multiple_of((1 - core) * 512, 512)

    def half(slot, ranges, first, start):
        r = None if first else acc[slot, pl.ds(start, 512), :]
        for lo, hi in ranges:
            term = jnp.dot(t_v[pl.ds(start, 512), lo:hi], q[slot, lo:hi, :], preferred_element_type=f32)
            r = term if r is None else r + term
        acc[slot, pl.ds(start, 512), :] = r

    def multiply(slot, ranges, first):
        def tile(i, c):
            half(slot, ranges, first, pl.multiple_of(i * 512, 512))
            return c

        lax.fori_loop(0, 2, tile, 0)

    def exchange(slot):
        return pltpu.make_async_remote_copy(
            src_ref=acc.at[slot, pl.ds(theirs, 512)], dst_ref=cx.at[slot], send_sem=cx_ssem.at[slot],
            recv_sem=cx_rsem.at[slot], device_id=sibling, device_id_type=MESH,
        )

    def scatter(slot):
        exchange(slot).wait_recv()
        rs_send[slot] = (acc[slot, pl.ds(mine, 512), :] + cx[slot]).astype(bf16)
        count, size = (16, 32) if slot == LAST else (8, 64)
        here = me if slot == LAST else z

        def one(n, c):
            k = far(n, count)
            to = lax.rem(here + k, count)
            target = to * 2 + core if slot == LAST else to * 4 + xl * 2 + core
            pltpu.make_async_remote_copy(
                src_ref=rs_send.at[slot, pl.ds(pl.multiple_of(to * size, size), size)],
                dst_ref=rs_recv.at[slot, pl.ds(pl.multiple_of((k - 1) * size, size), size)],
                send_sem=rs_ssem.at[slot], recv_sem=rs_rsem.at[slot],
                device_id=(group, target), device_id_type=MESH,
            ).start()
            return c

        lax.fori_loop(0, count - 1, one, 0, unroll=count - 1)

    def scattered(slot):
        landed = rs_recv.at[slot, pl.ds(0, 480 if slot == LAST else 448)]
        return pltpu.make_async_remote_copy(
            src_ref=landed, dst_ref=landed, send_sem=rs_ssem.at[slot], recv_sem=rs_rsem.at[slot],
            device_id=up, device_id_type=MESH,
        )

    def summed(slot, size):
        scattered(slot).wait_recv()
        own = pl.multiple_of((me if slot == LAST else z) * size, size)
        total = acc[slot, pl.ds(mine + own, size), :] + cx[slot, pl.ds(own, size), :]
        for k in range(512 // size - 1):
            total = total + rs_recv[slot, k * size : k * size + size, :].astype(f32)
        return total

    def swap(slot):
        return pltpu.make_async_remote_copy(
            src_ref=zs.at[slot, pl.ds(pl.multiple_of((1 - xl) * 32, 32), 32)], dst_ref=xs.at[slot],
            send_sem=xs_ssem.at[slot], recv_sem=xs_rsem.at[slot],
            device_id=(group, z * 4 + (1 - xl) * 2 + core), device_id_type=MESH,
        )

    def zsum(slot):
        zs[slot] = summed(slot, 64)

    def collect(slot):
        if slot == LAST:
            total = summed(slot, 32)
        else:
            swap(slot).wait_recv()
            total = zs[slot, pl.ds(pl.multiple_of(xl * 32, 32), 32), :] + xs[slot]
        placed = None
        for half in split(total):
            none = jnp.zeros_like(half)
            spread = jnp.concatenate(
                [jnp.concatenate([half if m == k else none for m in range(4)], axis=1) for k in range(4)], axis=0
            )
            term = lax.dot_general(hot[slot], spread, (((1,), (1,)), ((), ())), preferred_element_type=f32)
            placed = term if placed is None else placed + term
        placed = placed.reshape(32, 8, 128)
        a_send[...] = placed if slot == 0 else a_send[...] + placed

    def piece(slot, name, first):
        arrive(slot, name)
        multiply(slot, (PIECES[name],), first)

    load_t.wait()
    multiply(0, ((0, 4096),), True)
    exchange(0).start()

    def neighbours_b(above, below):
        arrive(3, "b" + above)
        arrive(1, "b" + below)
        if above in "01":
            send(3, "b" + above, up, 2)
            send(1, "b" + below, down, 2)
        send(3, "b" + above, across, 7)
        send(1, "b" + below, across, 5)

    def partner_a(n):
        arrive(4, "a" + n)
        send(4, "a" + n, up, 7)
        send(4, "a" + n, down, 5)

    def neighbours_a(above, below):
        arrive(3, "a" + above)
        arrive(1, "a" + below)
        if above in "01":
            send(3, "a" + above, up, 2)
            send(1, "a" + below, down, 2)

    def second_a(above, below):
        arrive(7, "a" + above)
        arrive(5, "a" + below)
        if above in "01":
            send(7, "a" + above, up, 6)
            send(5, "a" + below, down, 6)

    neighbours_b("0", "2")
    neighbours_b("1", "3")
    for above, below in zip(UP, DOWN):
        send(0, "a" + above, up, 3)
        send(0, "a" + below, down, 1)
    partner_a("0")
    scatter(0)
    partner_a("1")
    neighbours_b("2", "0")
    neighbours_b("3", "1")
    partner_a("2")

    for copy in id_copies:
        copy.wait_recv()
    rows = lax.broadcasted_iota(jnp.int32, (256, 128), 0)
    rows = rows // 8 * 32 + rows % 8
    for s in range(8):
        for k in range(4):
            same = rows + 8 * k == ids[s]
            hot[s, :, k * 128 : k * 128 + 128] = jnp.where(same, 1.0, 0.0).astype(bf16)

    partner_a("3")
    multiply(4, A, True)
    for n in "0213":
        arrive(2, "b" + n)
        send(2, "b" + n, across, 6)
    multiply(3, B, True)
    multiply(1, B, True)
    neighbours_a("0", "2")
    multiply(2, B, True)
    neighbours_a("1", "3")
    for n in "0123":
        arrive(4, "b" + n)
    multiply(4, B, False)
    exchange(4).start()
    zsum(0)
    neighbours_a("2", "0")
    scatter(4)
    neighbours_a("3", "1")
    multiply(3, A, False)
    exchange(3).start()
    multiply(1, A, False)
    exchange(1).start()
    second_a("0", "2")
    scatter(3)
    second_a("1", "3")
    scatter(1)
    zsum(4)
    second_a("2", "0")
    second_a("3", "1")
    multiply(7, A, True)
    multiply(5, A, True)
    zsum(3)
    for n in "0123":
        arrive(7, "b" + n)
    multiply(7, B, False)
    exchange(7).start()
    for n in "0123":
        arrive(5, "b" + n)
    multiply(5, B, False)
    exchange(5).start()
    zsum(1)
    for n in "0213":
        arrive(2, "a" + n)
    scatter(7)
    multiply(2, A, False)
    exchange(2).start()
    scatter(5)
    for slot in (0, 4, 3, 1):
        swap(slot).start()
    piece(6, "b0", True)
    piece(6, "b2", False)
    scatter(2)
    piece(6, "a0", False)
    piece(6, "a2", False)
    piece(6, "b1", False)
    piece(6, "b3", False)
    piece(6, "a1", False)
    arrive(6, "a3")
    half(6, (PIECES["a3"],), False, theirs)
    exchange(6).start()
    half(6, (PIECES["a3"],), False, mine)
    zsum(7)
    swap(7).start()
    collect(0)
    scatter(6)
    zsum(5)
    swap(5).start()
    zsum(2)
    swap(2).start()
    collect(4)
    collect(3)
    collect(1)
    collect(7)
    collect(5)
    collect(2)
    collect(6)

    place = core * 16 + me

    def deal(n, c):
        to = lax.rem(layer + far(n, 32), 32)
        pltpu.make_async_remote_copy(
            src_ref=a_send.at[to], dst_ref=a_recv.at[place], send_sem=a_ssem.at[0], recv_sem=a_rsem.at[0],
            device_id=(group, to), device_id_type=MESH,
        ).start()
        return c

    lax.fori_loop(0, 31, deal, 0, unroll=31)
    a_recv[place] = a_send[layer]
    dealt = pltpu.make_async_remote_copy(
        src_ref=a_recv.at[pl.ds(0, 31)], dst_ref=a_recv.at[pl.ds(0, 31)], send_sem=a_ssem.at[0], recv_sem=a_rsem.at[0],
        device_id=up, device_id_type=MESH,
    )
    for copy in sends:
        copy.wait_send()
    for copy in id_copies:
        copy.wait_send()
    for slot in range(8):
        exchange(slot).wait_send()
        scattered(slot).wait_send()
        if slot != LAST:
            swap(slot).wait_send()
    dealt.wait_recv()
    for m in range(8):
        tiles = [a_recv[4 * m + n] for n in range(4)]
        for k in range(4):
            out_ref[8 * k : 8 * k + 8, 128 * m : 128 * m + 128] = jnp.concatenate(
                [tile[:, 32 * k : 32 * k + 32] for tile in tiles], axis=1
            )

    dealt.wait_send()


def on_device(query_grads, query_ids, train_feats, basis_out, basis_in, eigen_vals):
    anywhere = pl.BlockSpec(memory_space=pl.ANY)
    vmem = pl.BlockSpec(memory_space=pltpu.VMEM)
    dma = pltpu.SemaphoreType.DMA
    return pl.pallas_call(
        kernel,
        out_shape=jax.ShapeDtypeStruct((32, 1024), f32),
        in_specs=[anywhere, vmem, anywhere, vmem, vmem, vmem],
        out_specs=vmem,
        scratch_shapes=[
            pltpu.VMEM((128, 4096), bf16),
            pltpu.VMEM((1024, 4096), bf16),
            pltpu.VMEM((8, 4096, 128), bf16),
            pltpu.VMEM((64 * PITCH, 128), f32),
            pltpu.VMEM((64 * PITCH, 128), f32),
            pltpu.VMEM((4096, 128), f32),
            pltpu.VMEM((4, 512, 256), bf16),
            pltpu.VMEM((8, 1024, 128), f32),
            pltpu.VMEM((8, 512, 128), f32),
            pltpu.VMEM((8, 512, 128), bf16),
            pltpu.VMEM((8, 480, 128), bf16),
            pltpu.VMEM((8, 64, 128), f32),
            pltpu.VMEM((8, 32, 128), f32),
            pltpu.VMEM((8, 1, 128), jnp.int32),
            pltpu.VMEM((8, 256, 512), bf16),
            pltpu.VMEM((32, 8, 128), f32),
            pltpu.VMEM((32, 8, 128), f32),
            dma((2,)),
            dma((56,)),
            dma((64,)),
            dma((8,)),
            dma((8,)),
            dma((8,)),
            dma((8,)),
            dma((8,)),
            dma((8,)),
            dma((8,)),
            dma((8,)),
            dma((1,)),
            dma((1,)),
        ],
        compiler_params=pltpu.CompilerParams(
            collective_id=0, has_side_effects=True, vmem_limit_bytes=48 * 2**20
        ),
        name="influence",
    )(
        *(
            pltpu.with_memory_space_constraint(x, pltpu.HBM)
            for x in (
                query_grads, query_ids.reshape(1, 128), train_feats, basis_out[0], basis_in[0], eigen_vals[0]
            )
        )
    ) * (1.0 / math.sqrt(131072))


def solution(mesh):
    return jax.shard_map(
        on_device,
        mesh=mesh,
        in_specs=(
            P("group", "layer"),
            P("group"),
            P("group", "layer"),
            P("layer", None, None),
            P("layer", None, None),
            P("layer", None, None),
        ),
        out_specs=P("layer", "group"),
        check_vma=False,
    )
```

```python
import functools
import math

import jax
import jax.numpy as jnp
from jax import lax
from jax.experimental import pallas as pl
from jax.experimental.pallas import tpu as pltpu
from jax.sharding import PartitionSpec as P

damping = 0.1
MESH = pl.DeviceIdType.MESH
f32, bf16 = jnp.float32, jnp.bfloat16

ORDER = (
    ("a0", 512), ("b0", 384), ("b2", 384), ("a1", 640), ("a2", 512), ("b1", 512), ("b3", 512), ("a3", 640),
)
PIECES = {}
row = 0
for name, size in ORDER:
    PIECES[name] = (row, row + size)
    row += size
NAMES = list(PIECES)
A = ((0, 512), (1280, 2432), (3456, 4096))
B = ((512, 1280), (2432, 3456))
UP = ("0", "1", "2", "3")
LAST = 6
PITCH = 72
DOWN = ("2", "3", "0", "1")


def split(x):
    high = x.astype(bf16)
    return high, (x - high.astype(f32)).astype(bf16)


def diagonal(block):
    width = block.shape[0]
    four = jnp.concatenate([block] * 4, axis=1)
    four = jnp.concatenate([four] * 4, axis=0)
    rows = lax.broadcasted_iota(jnp.int32, four.shape, 0) // width
    cols = lax.broadcasted_iota(jnp.int32, four.shape, 1) // width
    return jnp.where(rows == cols, four, 0.0)


def far(n, count):
    return count // 2 + (n % 2 * 2 - 1) * ((n + 1) // 2)


def apply_basis(matrix, x):
    high, low = split(x)
    both = jnp.dot(matrix, high, preferred_element_type=f32)
    rest = jnp.dot(matrix[:256], low, preferred_element_type=f32)
    return both[:256] + both[256:] + rest


def kernel(
    g_hbm, ids_ref, t_hbm, bo_ref, bi_ref, eig_ref, out_ref,
    g_v, t_v, q, y1, y2, inv, bdm, acc, cx, rs_send, rs_recv, zs, xs, ids, hot, a_send, a_round, a_recv,
    load_sem, q_send, q_recv, id_send, id_recv, cx_ssem, cx_rsem, rs_ssem, rs_rsem, xs_ssem, xs_rsem, a_ssem, a_rsem,
):
    group, layer = lax.axis_index("group"), lax.axis_index("layer")
    xh, y = group // 4, group % 4
    me, core = layer // 2, layer % 2
    z, xl = me // 2, me % 2
    up = (xh * 4 + lax.rem(y + 1, 4), layer)
    down = (xh * 4 + lax.rem(y + 3, 4), layer)
    across = ((1 - xh) * 4 + y, layer)
    sibling = (group, me * 2 + 1 - core)

    load_g = pltpu.make_async_copy(g_hbm, g_v, load_sem.at[0])
    load_t = pltpu.make_async_copy(t_hbm, t_v, load_sem.at[1])
    load_g.start()

    barrier = pltpu.get_barrier_semaphore()

    def greet_group(k, c):
        pl.semaphore_signal(barrier, inc=1, device_id=(lax.rem(group + k, 8), layer), device_id_type=MESH)
        return c

    def greet_layer(n, c):
        to = lax.rem(layer + far(n, 32), 32)
        pl.semaphore_signal(barrier, inc=1, device_id=(group, to), device_id_type=MESH)
        return c

    lax.fori_loop(0, 31, greet_layer, 0, unroll=31)
    lax.fori_loop(1, 8, greet_group, 0, unroll=7)
    load_t.start()

    bo = diagonal(bo_ref[...])
    bi = diagonal(bi_ref[...])
    for place, matrix in enumerate((bi.T, bo.T, bo, bi)):
        high, low = split(matrix)
        bdm[place, 0:256, :] = high
        bdm[place, 256:512, :] = low
    scale = 1.0 / (eig_ref[...] + damping)
    for j in range(64):
        inv[j * 64 : j * 64 + 64, :] = jnp.broadcast_to(scale[:, j : j + 1], (64, 128))

    load_g.wait()

    def spread(ref, u, r):
        for h in range(2):
            for s in range(4):
                start = pl.multiple_of((u * 8 + h * 4 + s) * PITCH, 8)
                ref[pl.ds(start, 64), :] = r[s * 64 : s * 64 + 64, h * 128 : h * 128 + 128]

    def stage_a(u, c):
        base = pl.multiple_of(u * 512, 512)
        left = g_v[:, pl.ds(base, 256)]
        right = g_v[:, pl.ds(base + 256, 256)]
        both = lax.dot_general(
            bdm[0], jnp.concatenate([left, right], axis=0), (((1,), (1,)), ((), ())), preferred_element_type=f32
        )
        r = both[:256] + both[256:]
        spread(y1, u, r)
        return c

    def strided(ref, u):
        halves = []
        for h in range(2):
            halves.append(
                jnp.concatenate([ref[pl.ds(u * 8 + h * 4 + s, 64, stride=PITCH), :] for s in range(4)], axis=0)
            )
        return jnp.concatenate(halves, axis=1)

    def stage_bc(u, c):
        base = pl.multiple_of(u * 512, 512)
        r = apply_basis(bdm[1], strided(y1, u))
        r = r * jnp.concatenate([inv[pl.ds(base, 256), :], inv[pl.ds(base + 256, 256), :]], axis=1)
        r = apply_basis(bdm[2], r)
        spread(y2, u, r)
        return c

    def stage_d(u, c):
        base = pl.multiple_of(u * 512, 512)
        r = apply_basis(bdm[3], strided(y2, u)).astype(bf16)
        q[0, pl.ds(base, 256), :] = r[:, :128]
        q[0, pl.ds(base + 256, 256), :] = r[:, 128:]
        return c

    lax.fori_loop(0, 8, stage_a, 0, unroll=8)
    lax.fori_loop(0, 8, stage_bc, 0, unroll=8)
    lax.fori_loop(0, 3, stage_d, 0, unroll=3)

    pl.semaphore_wait(barrier, 38)

    sends = []

    def send(src_slot, piece, target, dst_slot):
        lo, hi = PIECES[piece]
        copy = pltpu.make_async_remote_copy(
            src_ref=q.at[src_slot, pl.ds(lo, hi - lo)],
            dst_ref=q.at[dst_slot, pl.ds(lo, hi - lo)],
            send_sem=q_send.at[len(sends)],
            recv_sem=q_recv.at[dst_slot * 8 + NAMES.index(piece)],
            device_id=target,
            device_id_type=MESH,
        )
        copy.start()
        sends.append(copy)

    def arrive(slot, piece):
        lo, hi = PIECES[piece]
        part = q.at[slot, pl.ds(lo, hi - lo)]
        pltpu.make_async_remote_copy(
            src_ref=part, dst_ref=part, send_sem=q_send.at[0], recv_sem=q_recv.at[slot * 8 + NAMES.index(piece)],
            device_id=up, device_id_type=MESH,
        ).wait_recv()

    send(0, "a0", across, 4)
    send(0, "b0", up, 3)
    send(0, "b2", down, 1)
    lax.fori_loop(3, 8, stage_d, 0, unroll=5)
    for n in "123":
        send(0, "a" + n, across, 4)
    for above, below in zip(UP[1:], DOWN[1:]):
        send(0, "b" + above, up, 3)
        send(0, "b" + below, down, 1)
    for n in "0123":
        send(0, "b" + n, across, 4)

    def id_target(k):
        return (lax.rem(xh + k // 4, 2) * 4 + lax.rem(y + k, 4), layer)

    def id_slot(k):
        return k // 4 * 4 + (4 - k % 4) % 4

    id_copies = []
    for k in range(1, 8):
        copy = pltpu.make_async_remote_copy(
            src_ref=ids_ref, dst_ref=ids.at[id_slot(k)], send_sem=id_send.at[id_slot(k)], recv_sem=id_recv.at[id_slot(k)],
            device_id=id_target(k), device_id_type=MESH,
        )
        copy.start()
        id_copies.append(copy)
    ids[0] = ids_ref[...]

    mine = pl.multiple_of(core * 512, 512)
    theirs = pl.multiple_of((1 - core) * 512, 512)

    def half(slot, ranges, first, start):
        r = None if first else acc[slot, pl.ds(start, 512), :]
        for lo, hi in ranges:
            term = jnp.dot(t_v[pl.ds(start, 512), lo:hi], q[slot, lo:hi, :], preferred_element_type=f32)
            r = term if r is None else r + term
        acc[slot, pl.ds(start, 512), :] = r

    def multiply(slot, ranges, first):
        def tile(i, c):
            half(slot, ranges, first, pl.multiple_of(i * 512, 512))
            return c

        lax.fori_loop(0, 2, tile, 0)

    def exchange(slot):
        return pltpu.make_async_remote_copy(
            src_ref=acc.at[slot, pl.ds(theirs, 512)], dst_ref=cx.at[slot], send_sem=cx_ssem.at[slot],
            recv_sem=cx_rsem.at[slot], device_id=sibling, device_id_type=MESH,
        )

    def scatter(slot):
        exchange(slot).wait_recv()
        rs_send[slot] = (acc[slot, pl.ds(mine, 512), :] + cx[slot]).astype(bf16)
        count, size = (16, 32) if slot == LAST else (8, 64)
        here = me if slot == LAST else z

        def one(n, c):
            k = far(n, count)
            to = lax.rem(here + k, count)
            target = to * 2 + core if slot == LAST else to * 4 + xl * 2 + core
            pltpu.make_async_remote_copy(
                src_ref=rs_send.at[slot, pl.ds(pl.multiple_of(to * size, size), size)],
                dst_ref=rs_recv.at[slot, pl.ds(pl.multiple_of((k - 1) * size, size), size)],
                send_sem=rs_ssem.at[slot], recv_sem=rs_rsem.at[slot],
                device_id=(group, target), device_id_type=MESH,
            ).start()
            return c

        lax.fori_loop(0, count - 1, one, 0, unroll=count - 1)

    def scattered(slot):
        landed = rs_recv.at[slot, pl.ds(0, 480 if slot == LAST else 448)]
        return pltpu.make_async_remote_copy(
            src_ref=landed, dst_ref=landed, send_sem=rs_ssem.at[slot], recv_sem=rs_rsem.at[slot],
            device_id=up, device_id_type=MESH,
        )

    def summed(slot, size):
        scattered(slot).wait_recv()
        own = pl.multiple_of((me if slot == LAST else z) * size, size)
        total = acc[slot, pl.ds(mine + own, size), :] + cx[slot, pl.ds(own, size), :]
        for k in range(512 // size - 1):
            total = total + rs_recv[slot, k * size : k * size + size, :].astype(f32)
        return total

    def swap(slot):
        return pltpu.make_async_remote_copy(
            src_ref=zs.at[slot, pl.ds(pl.multiple_of((1 - xl) * 32, 32), 32)], dst_ref=xs.at[slot],
            send_sem=xs_ssem.at[slot], recv_sem=xs_rsem.at[slot],
            device_id=(group, z * 4 + (1 - xl) * 2 + core), device_id_type=MESH,
        )

    def zsum(slot):
        zs[slot] = summed(slot, 64)

    def collect(slot):
        if slot == LAST:
            total = summed(slot, 32)
        else:
            swap(slot).wait_recv()
            total = zs[slot, pl.ds(pl.multiple_of(xl * 32, 32), 32), :] + xs[slot]
        spread = []
        for half_total in split(total):
            none = jnp.zeros_like(half_total)
            spread.append(
                jnp.concatenate(
                    [jnp.concatenate([half_total if m == k else none for m in range(4)], axis=1) for k in range(4)],
                    axis=0,
                )
            )
        placed = lax.dot_general(
            jnp.concatenate([hot[slot], hot[slot]], axis=1), jnp.concatenate(spread, axis=1),
            (((1,), (1,)), ((), ())), preferred_element_type=f32,
        )
        placed = placed.reshape(32, 8, 128)
        a_send[...] = placed if slot == 0 else a_send[...] + placed

    def piece(slot, name, first):
        arrive(slot, name)
        multiply(slot, (PIECES[name],), first)

    load_t.wait()
    multiply(0, ((0, 4096),), True)
    exchange(0).start()

    def neighbours_b(above, below):
        arrive(3, "b" + above)
        arrive(1, "b" + below)
        if above in "01":
            send(3, "b" + above, up, 2)
            send(1, "b" + below, down, 2)
        send(3, "b" + above, across, 7)
        send(1, "b" + below, across, 5)

    def partner_a(n):
        arrive(4, "a" + n)
        send(4, "a" + n, up, 7)
        send(4, "a" + n, down, 5)

    def neighbours_a(above, below):
        arrive(3, "a" + above)
        arrive(1, "a" + below)
        if above in "01":
            send(3, "a" + above, up, 2)
            send(1, "a" + below, down, 2)

    def second_a(above, below):
        arrive(7, "a" + above)
        arrive(5, "a" + below)
        if above in "01":
            send(7, "a" + above, up, 6)
            send(5, "a" + below, down, 6)

    neighbours_b("0", "2")
    neighbours_b("1", "3")
    for above, below in zip(UP, DOWN):
        send(0, "a" + above, up, 3)
        send(0, "a" + below, down, 1)
    partner_a("0")
    scatter(0)
    partner_a("1")
    neighbours_b("2", "0")
    neighbours_b("3", "1")
    partner_a("2")

    for copy in id_copies:
        copy.wait_recv()
    rows = lax.broadcasted_iota(jnp.int32, (256, 128), 0)
    rows = rows // 8 * 32 + rows % 8
    for s in range(8):
        for k in range(4):
            same = rows + 8 * k == ids[s]
            hot[s, :, k * 128 : k * 128 + 128] = jnp.where(same, 1.0, 0.0).astype(bf16)

    partner_a("3")
    multiply(4, A, True)
    for n in "0213":
        arrive(2, "b" + n)
        send(2, "b" + n, across, 6)
    multiply(3, B, True)
    multiply(1, B, True)
    neighbours_a("0", "2")
    multiply(2, B, True)
    neighbours_a("1", "3")
    for n in "0123":
        arrive(4, "b" + n)
    multiply(4, B, False)
    exchange(4).start()
    zsum(0)
    neighbours_a("2", "0")
    scatter(4)
    neighbours_a("3", "1")
    multiply(3, A, False)
    exchange(3).start()
    multiply(1, A, False)
    exchange(1).start()
    second_a("0", "2")
    scatter(3)
    second_a("1", "3")
    scatter(1)
    zsum(4)
    second_a("2", "0")
    second_a("3", "1")
    multiply(7, A, True)
    multiply(5, A, True)
    zsum(3)
    for n in "0123":
        arrive(7, "b" + n)
    multiply(7, B, False)
    exchange(7).start()
    for n in "0123":
        arrive(5, "b" + n)
    multiply(5, B, False)
    exchange(5).start()
    zsum(1)
    for n in "0213":
        arrive(2, "a" + n)
    scatter(7)
    multiply(2, A, False)
    exchange(2).start()
    scatter(5)
    for slot in (0, 4, 3, 1):
        swap(slot).start()
    piece(6, "b0", True)
    piece(6, "b2", False)
    scatter(2)
    piece(6, "a0", False)
    piece(6, "a2", False)
    piece(6, "b1", False)
    piece(6, "b3", False)
    piece(6, "a1", False)
    arrive(6, "a3")
    half(6, (PIECES["a3"],), False, theirs)
    exchange(6).start()
    half(6, (PIECES["a3"],), False, mine)
    collect(0)
    collect(4)
    scatter(6)
    for slot in (7, 5, 2):
        zsum(slot)
        swap(slot).start()
    collect(3)
    collect(1)
    collect(7)
    collect(5)
    collect(2)
    collect(6)

    place = core * 16 + me
    a_round[...] = a_send[...].astype(bf16)

    def deal(n, c):
        to = lax.rem(layer + far(n, 32), 32)
        pltpu.make_async_remote_copy(
            src_ref=a_round.at[to], dst_ref=a_recv.at[place], send_sem=a_ssem.at[0], recv_sem=a_rsem.at[0],
            device_id=(group, to), device_id_type=MESH,
        ).start()
        return c

    lax.fori_loop(0, 31, deal, 0, unroll=31)
    a_recv[place] = a_round[layer]
    dealt = pltpu.make_async_remote_copy(
        src_ref=a_recv.at[pl.ds(0, 31)], dst_ref=a_recv.at[pl.ds(0, 31)], send_sem=a_ssem.at[0], recv_sem=a_rsem.at[0],
        device_id=up, device_id_type=MESH,
    )
    for copy in sends:
        copy.wait_send()
    for copy in id_copies:
        copy.wait_send()
    for slot in range(8):
        exchange(slot).wait_send()
        scattered(slot).wait_send()
        if slot != LAST:
            swap(slot).wait_send()
    dealt.wait_recv()
    for m in range(8):
        tiles = [a_recv[4 * m + n].astype(f32) for n in range(4)]
        for k in range(4):
            out_ref[8 * k : 8 * k + 8, 128 * m : 128 * m + 128] = jnp.concatenate(
                [tile[:, 32 * k : 32 * k + 32] for tile in tiles], axis=1
            )

    dealt.wait_send()


def on_device(query_grads, query_ids, train_feats, basis_out, basis_in, eigen_vals):
    anywhere = pl.BlockSpec(memory_space=pl.ANY)
    vmem = pl.BlockSpec(memory_space=pltpu.VMEM)
    dma = pltpu.SemaphoreType.DMA
    return pl.pallas_call(
        kernel,
        out_shape=jax.ShapeDtypeStruct((32, 1024), f32),
        in_specs=[anywhere, vmem, anywhere, vmem, vmem, vmem],
        out_specs=vmem,
        scratch_shapes=[
            pltpu.VMEM((128, 4096), bf16),
            pltpu.VMEM((1024, 4096), bf16),
            pltpu.VMEM((8, 4096, 128), bf16),
            pltpu.VMEM((64 * PITCH, 128), f32),
            pltpu.VMEM((64 * PITCH, 128), f32),
            pltpu.VMEM((4096, 128), f32),
            pltpu.VMEM((4, 512, 256), bf16),
            pltpu.VMEM((8, 1024, 128), f32),
            pltpu.VMEM((8, 512, 128), f32),
            pltpu.VMEM((8, 512, 128), bf16),
            pltpu.VMEM((8, 480, 128), bf16),
            pltpu.VMEM((8, 64, 128), f32),
            pltpu.VMEM((8, 32, 128), f32),
            pltpu.VMEM((8, 1, 128), jnp.int32),
            pltpu.VMEM((8, 256, 512), bf16),
            pltpu.VMEM((32, 8, 128), f32),
            pltpu.VMEM((32, 8, 128), bf16),
            pltpu.VMEM((32, 8, 128), bf16),
            dma((2,)),
            dma((56,)),
            dma((64,)),
            dma((8,)),
            dma((8,)),
            dma((8,)),
            dma((8,)),
            dma((8,)),
            dma((8,)),
            dma((8,)),
            dma((8,)),
            dma((1,)),
            dma((1,)),
        ],
        compiler_params=pltpu.CompilerParams(
            collective_id=0, has_side_effects=True, vmem_limit_bytes=48 * 2**20
        ),
        name="influence",
    )(
        *(
            pltpu.with_memory_space_constraint(x, pltpu.HBM)
            for x in (
                query_grads, query_ids.reshape(1, 128), train_feats, basis_out[0], basis_in[0], eigen_vals[0]
            )
        )
    ) * (1.0 / math.sqrt(131072))


def solution(mesh):
    return jax.shard_map(
        on_device,
        mesh=mesh,
        in_specs=(
            P("group", "layer"),
            P("group"),
            P("group", "layer"),
            P("layer", None, None),
            P("layer", None, None),
            P("layer", None, None),
        ),
        out_specs=P("layer", "group"),
        check_vma=False,
    )
```

```python
import functools
import math

import jax
import jax.numpy as jnp
from jax import lax
from jax.experimental import pallas as pl
from jax.experimental.pallas import tpu as pltpu
from jax.sharding import PartitionSpec as P

damping = 0.1
MESH = pl.DeviceIdType.MESH
f32, bf16 = jnp.float32, jnp.bfloat16

ORDER = (
    ("a0", 512), ("b0", 384), ("b2", 384), ("a1", 640), ("a2", 512), ("b1", 512), ("b3", 512), ("a3", 640),
)
PIECES = {}
row = 0
for name, size in ORDER:
    PIECES[name] = (row, row + size)
    row += size
NAMES = list(PIECES)
A = ((0, 512), (1280, 2432), (3456, 4096))
B = ((512, 1280), (2432, 3456))
UP = ("0", "1", "2", "3")
LAST = 6
PITCH = 72
DOWN = ("2", "3", "0", "1")


def split(x):
    high = x.astype(bf16)
    return high, (x - high.astype(f32)).astype(bf16)


def diagonal(block):
    width = block.shape[0]
    four = jnp.concatenate([block] * 4, axis=1)
    four = jnp.concatenate([four] * 4, axis=0)
    rows = lax.broadcasted_iota(jnp.int32, four.shape, 0) // width
    cols = lax.broadcasted_iota(jnp.int32, four.shape, 1) // width
    return jnp.where(rows == cols, four, 0.0)


def far(n, count):
    return count // 2 + (n % 2 * 2 - 1) * ((n + 1) // 2)


def apply_basis(matrix, x):
    high, low = split(x)
    both = jnp.dot(matrix, high, preferred_element_type=f32)
    rest = jnp.dot(matrix[:256], low, preferred_element_type=f32)
    return both[:256] + both[256:] + rest


def kernel(
    g_hbm, ids_ref, t_hbm, bo_ref, bi_ref, eig_ref, out_ref,
    g_v, t_v, q, y1, y2, inv, bdm, acc, cx, rs_send, rs_recv, zs, xs, ids, hot, a_send, a_round, a_recv,
    load_sem, q_send, q_recv, id_send, id_recv, cx_ssem, cx_rsem, rs_ssem, rs_rsem, xs_ssem, xs_rsem, a_ssem, a_rsem,
):
    group, layer = lax.axis_index("group"), lax.axis_index("layer")
    xh, y = group // 4, group % 4
    me, core = layer // 2, layer % 2
    z, xl = me // 2, me % 2
    up = (xh * 4 + lax.rem(y + 1, 4), layer)
    down = (xh * 4 + lax.rem(y + 3, 4), layer)
    across = ((1 - xh) * 4 + y, layer)
    sibling = (group, me * 2 + 1 - core)

    load_g = pltpu.make_async_copy(g_hbm, g_v, load_sem.at[0])
    load_t = pltpu.make_async_copy(t_hbm, t_v, load_sem.at[1])
    load_g.start()

    barrier = pltpu.get_barrier_semaphore()

    def greet_group(k, c):
        pl.semaphore_signal(barrier, inc=1, device_id=(lax.rem(group + k, 8), layer), device_id_type=MESH)
        return c

    def greet_layer(n, c):
        to = lax.rem(layer + far(n, 32), 32)
        pl.semaphore_signal(barrier, inc=1, device_id=(group, to), device_id_type=MESH)
        return c

    lax.fori_loop(0, 31, greet_layer, 0, unroll=31)
    lax.fori_loop(1, 8, greet_group, 0, unroll=7)
    load_t.start()

    bo = diagonal(bo_ref[...])
    bi = diagonal(bi_ref[...])
    for place, matrix in enumerate((bi.T, bo.T, bo, bi)):
        high, low = split(matrix)
        bdm[place, 0:256, :] = high
        bdm[place, 256:512, :] = low
    scale = 1.0 / (eig_ref[...] + damping)
    for j in range(64):
        inv[j * 64 : j * 64 + 64, :] = jnp.broadcast_to(scale[:, j : j + 1], (64, 128))

    load_g.wait()

    def spread(ref, u, r):
        for h in range(2):
            for s in range(4):
                start = pl.multiple_of((u * 8 + h * 4 + s) * PITCH, 8)
                ref[pl.ds(start, 64), :] = r[s * 64 : s * 64 + 64, h * 128 : h * 128 + 128]

    def stage_a(u, c):
        base = pl.multiple_of(u * 512, 512)
        left = g_v[:, pl.ds(base, 256)]
        right = g_v[:, pl.ds(base + 256, 256)]
        both = lax.dot_general(
            bdm[0], jnp.concatenate([left, right], axis=0), (((1,), (1,)), ((), ())), preferred_element_type=f32
        )
        r = both[:256] + both[256:]
        spread(y1, u, r)
        return c

    def strided(ref, u):
        halves = []
        for h in range(2):
            halves.append(
                jnp.concatenate([ref[pl.ds(u * 8 + h * 4 + s, 64, stride=PITCH), :] for s in range(4)], axis=0)
            )
        return jnp.concatenate(halves, axis=1)

    def stage_bc(u, c):
        base = pl.multiple_of(u * 512, 512)
        r = apply_basis(bdm[1], strided(y1, u))
        r = r * jnp.concatenate([inv[pl.ds(base, 256), :], inv[pl.ds(base + 256, 256), :]], axis=1)
        r = apply_basis(bdm[2], r)
        spread(y2, u, r)
        return c

    def stage_d(u, c):
        base = pl.multiple_of(u * 512, 512)
        r = apply_basis(bdm[3], strided(y2, u)).astype(bf16)
        q[0, pl.ds(base, 256), :] = r[:, :128]
        q[0, pl.ds(base + 256, 256), :] = r[:, 128:]
        return c

    lax.fori_loop(0, 8, stage_a, 0, unroll=8)
    lax.fori_loop(0, 8, stage_bc, 0, unroll=8)
    lax.fori_loop(0, 3, stage_d, 0, unroll=3)

    pl.semaphore_wait(barrier, 38)

    sends = []

    def send(src_slot, piece, target, dst_slot):
        lo, hi = PIECES[piece]
        copy = pltpu.make_async_remote_copy(
            src_ref=q.at[src_slot, pl.ds(lo, hi - lo)],
            dst_ref=q.at[dst_slot, pl.ds(lo, hi - lo)],
            send_sem=q_send.at[len(sends)],
            recv_sem=q_recv.at[dst_slot * 8 + NAMES.index(piece)],
            device_id=target,
            device_id_type=MESH,
        )
        copy.start()
        sends.append(copy)

    def arrive(slot, piece):
        lo, hi = PIECES[piece]
        part = q.at[slot, pl.ds(lo, hi - lo)]
        pltpu.make_async_remote_copy(
            src_ref=part, dst_ref=part, send_sem=q_send.at[0], recv_sem=q_recv.at[slot * 8 + NAMES.index(piece)],
            device_id=up, device_id_type=MESH,
        ).wait_recv()

    send(0, "a0", across, 4)
    send(0, "b0", up, 3)
    send(0, "b2", down, 1)
    lax.fori_loop(3, 8, stage_d, 0, unroll=5)
    for n in "123":
        send(0, "a" + n, across, 4)
    for above, below in zip(UP[1:], DOWN[1:]):
        send(0, "b" + above, up, 3)
        send(0, "b" + below, down, 1)
    for n in "0123":
        send(0, "b" + n, across, 4)

    def id_target(k):
        return (lax.rem(xh + k // 4, 2) * 4 + lax.rem(y + k, 4), layer)

    def id_slot(k):
        return k // 4 * 4 + (4 - k % 4) % 4

    id_copies = []
    for k in range(1, 8):
        copy = pltpu.make_async_remote_copy(
            src_ref=ids_ref, dst_ref=ids.at[id_slot(k)], send_sem=id_send.at[id_slot(k)], recv_sem=id_recv.at[id_slot(k)],
            device_id=id_target(k), device_id_type=MESH,
        )
        copy.start()
        id_copies.append(copy)
    ids[0] = ids_ref[...]

    mine = pl.multiple_of(core * 512, 512)
    theirs = pl.multiple_of((1 - core) * 512, 512)

    def half(slot, ranges, first, start):
        r = None if first else acc[slot, pl.ds(start, 512), :]
        for lo, hi in ranges:
            term = jnp.dot(t_v[pl.ds(start, 512), lo:hi], q[slot, lo:hi, :], preferred_element_type=f32)
            r = term if r is None else r + term
        acc[slot, pl.ds(start, 512), :] = r

    def multiply(slot, ranges, first):
        def tile(i, c):
            half(slot, ranges, first, pl.multiple_of(i * 512, 512))
            return c

        lax.fori_loop(0, 2, tile, 0)

    def exchange(slot):
        return pltpu.make_async_remote_copy(
            src_ref=acc.at[slot, pl.ds(theirs, 512)], dst_ref=cx.at[slot], send_sem=cx_ssem.at[slot],
            recv_sem=cx_rsem.at[slot], device_id=sibling, device_id_type=MESH,
        )

    def scatter(slot):
        exchange(slot).wait_recv()
        rs_send[slot] = (acc[slot, pl.ds(mine, 512), :] + cx[slot]).astype(bf16)
        count, size = (16, 32) if slot == LAST else (8, 64)
        here = me if slot == LAST else z

        def one(n, c):
            k = far(n, count)
            to = lax.rem(here + k, count)
            target = to * 2 + core if slot == LAST else to * 4 + xl * 2 + core
            pltpu.make_async_remote_copy(
                src_ref=rs_send.at[slot, pl.ds(pl.multiple_of(to * size, size), size)],
                dst_ref=rs_recv.at[slot, pl.ds(pl.multiple_of((k - 1) * size, size), size)],
                send_sem=rs_ssem.at[slot], recv_sem=rs_rsem.at[slot],
                device_id=(group, target), device_id_type=MESH,
            ).start()
            return c

        lax.fori_loop(0, count - 1, one, 0, unroll=count - 1)

    def scattered(slot):
        landed = rs_recv.at[slot, pl.ds(0, 480 if slot == LAST else 448)]
        return pltpu.make_async_remote_copy(
            src_ref=landed, dst_ref=landed, send_sem=rs_ssem.at[slot], recv_sem=rs_rsem.at[slot],
            device_id=up, device_id_type=MESH,
        )

    def summed(slot, size):
        scattered(slot).wait_recv()
        own = pl.multiple_of((me if slot == LAST else z) * size, size)
        total = acc[slot, pl.ds(mine + own, size), :] + cx[slot, pl.ds(own, size), :]
        for k in range(512 // size - 1):
            total = total + rs_recv[slot, k * size : k * size + size, :].astype(f32)
        return total

    def swap(slot):
        return pltpu.make_async_remote_copy(
            src_ref=zs.at[slot, pl.ds(pl.multiple_of((1 - xl) * 32, 32), 32)], dst_ref=xs.at[slot],
            send_sem=xs_ssem.at[slot], recv_sem=xs_rsem.at[slot],
            device_id=(group, z * 4 + (1 - xl) * 2 + core), device_id_type=MESH,
        )

    def zsum(slot):
        zs[slot] = summed(slot, 64)

    def collect(slot):
        if slot == LAST:
            total = summed(slot, 32)
        else:
            swap(slot).wait_recv()
            total = zs[slot, pl.ds(pl.multiple_of(xl * 32, 32), 32), :] + xs[slot]
        spread = []
        for half_total in split(total):
            none = jnp.zeros_like(half_total)
            spread.append(
                jnp.concatenate(
                    [jnp.concatenate([half_total if m == k else none for m in range(4)], axis=1) for k in range(4)],
                    axis=0,
                )
            )
        placed = lax.dot_general(
            jnp.concatenate([hot[slot], hot[slot]], axis=1), jnp.concatenate(spread, axis=1),
            (((1,), (1,)), ((), ())), preferred_element_type=f32,
        )
        placed = placed.reshape(32, 8, 128)
        a_send[...] = placed if slot == 0 else a_send[...] + placed

    def piece(slot, name, first):
        arrive(slot, name)
        multiply(slot, (PIECES[name],), first)

    load_t.wait()
    multiply(0, ((0, 4096),), True)
    exchange(0).start()

    def neighbours_b(above, below):
        arrive(3, "b" + above)
        arrive(1, "b" + below)
        if above in "01":
            send(3, "b" + above, up, 2)
            send(1, "b" + below, down, 2)
        send(3, "b" + above, across, 7)
        send(1, "b" + below, across, 5)

    def partner_a(n):
        arrive(4, "a" + n)
        send(4, "a" + n, up, 7)
        send(4, "a" + n, down, 5)

    def neighbours_a(above, below):
        arrive(3, "a" + above)
        arrive(1, "a" + below)
        if above in "01":
            send(3, "a" + above, up, 2)
            send(1, "a" + below, down, 2)

    def second_a(above, below):
        arrive(7, "a" + above)
        arrive(5, "a" + below)
        if above in "01":
            send(7, "a" + above, up, 6)
            send(5, "a" + below, down, 6)

    neighbours_b("0", "2")
    neighbours_b("1", "3")
    for above, below in zip(UP, DOWN):
        send(0, "a" + above, up, 3)
        send(0, "a" + below, down, 1)
    partner_a("0")
    scatter(0)
    partner_a("1")
    neighbours_b("2", "0")
    neighbours_b("3", "1")
    partner_a("2")

    for copy in id_copies:
        copy.wait_recv()
    rows = lax.broadcasted_iota(jnp.int32, (256, 128), 0)
    rows = rows // 8 * 32 + rows % 8
    for s in range(8):
        for k in range(4):
            same = rows + 8 * k == ids[s]
            hot[s, :, k * 128 : k * 128 + 128] = jnp.where(same, 1.0, 0.0).astype(bf16)

    partner_a("3")
    multiply(4, A, True)
    for n in "0213":
        arrive(2, "b" + n)
        send(2, "b" + n, across, 6)
    multiply(3, B, True)
    multiply(1, B, True)
    neighbours_a("0", "2")
    multiply(2, B, True)
    neighbours_a("1", "3")
    for n in "0123":
        arrive(4, "b" + n)
    multiply(4, B, False)
    exchange(4).start()
    zsum(0)
    neighbours_a("2", "0")
    scatter(4)
    neighbours_a("3", "1")
    multiply(3, A, False)
    exchange(3).start()
    multiply(1, A, False)
    exchange(1).start()
    second_a("0", "2")
    scatter(3)
    second_a("1", "3")
    scatter(1)
    zsum(4)
    second_a("2", "0")
    second_a("3", "1")
    multiply(7, A, True)
    multiply(5, A, True)
    zsum(3)
    for n in "0123":
        arrive(7, "b" + n)
    multiply(7, B, False)
    exchange(7).start()
    for n in "0123":
        arrive(5, "b" + n)
    multiply(5, B, False)
    exchange(5).start()
    zsum(1)
    for n in "0213":
        arrive(2, "a" + n)
    scatter(7)
    multiply(2, A, False)
    exchange(2).start()
    scatter(5)
    for slot in (0, 4, 3, 1):
        swap(slot).start()
    piece(6, "b0", True)
    piece(6, "b2", False)
    scatter(2)
    piece(6, "a0", False)
    piece(6, "a2", False)
    piece(6, "b1", False)
    piece(6, "b3", False)
    piece(6, "a1", False)
    arrive(6, "a3")
    half(6, (PIECES["a3"],), False, theirs)
    exchange(6).start()
    half(6, (PIECES["a3"],), False, mine)
    collect(0)
    collect(4)
    scatter(6)
    for slot in (7, 5, 2):
        zsum(slot)
        swap(slot).start()
    collect(3)
    collect(1)
    collect(7)
    collect(5)
    collect(2)
    collect(6)

    place = core * 16 + me
    a_round[...] = a_send[...].astype(bf16)

    def deal(n, c):
        to = lax.rem(layer + far(n, 32), 32)
        pltpu.make_async_remote_copy(
            src_ref=a_round.at[to], dst_ref=a_recv.at[place], send_sem=a_ssem.at[0], recv_sem=a_rsem.at[0],
            device_id=(group, to), device_id_type=MESH,
        ).start()
        return c

    lax.fori_loop(0, 31, deal, 0, unroll=31)
    a_recv[place] = a_round[layer]
    dealt = pltpu.make_async_remote_copy(
        src_ref=a_recv.at[pl.ds(0, 31)], dst_ref=a_recv.at[pl.ds(0, 31)], send_sem=a_ssem.at[0], recv_sem=a_rsem.at[0],
        device_id=up, device_id_type=MESH,
    )
    for copy in sends:
        copy.wait_send()
    for copy in id_copies:
        copy.wait_send()
    for slot in range(8):
        exchange(slot).wait_send()
        scattered(slot).wait_send()
        if slot != LAST:
            swap(slot).wait_send()
    dealt.wait_recv()
    for m in range(8):
        tiles = [a_recv[4 * m + n].astype(f32) for n in range(4)]
        for k in range(4):
            out_ref[8 * k : 8 * k + 8, 128 * m : 128 * m + 128] = jnp.concatenate(
                [tile[:, 32 * k : 32 * k + 32] for tile in tiles], axis=1
            )

    dealt.wait_send()


def on_device(query_grads, query_ids, train_feats, basis_out, basis_in, eigen_vals):
    anywhere = pl.BlockSpec(memory_space=pl.ANY)
    vmem = pl.BlockSpec(memory_space=pltpu.VMEM)
    dma = pltpu.SemaphoreType.DMA
    return pl.pallas_call(
        kernel,
        out_shape=jax.ShapeDtypeStruct((32, 1024), f32),
        in_specs=[anywhere, vmem, anywhere, vmem, vmem, vmem],
        out_specs=vmem,
        scratch_shapes=[
            pltpu.VMEM((128, 4096), bf16),
            pltpu.VMEM((1024, 4096), bf16),
            pltpu.VMEM((8, 4096, 128), bf16),
            pltpu.VMEM((65 * PITCH, 128), f32),
            pltpu.VMEM((65 * PITCH, 128), f32),
            pltpu.VMEM((4096, 128), f32),
            pltpu.VMEM((4, 512, 256), bf16),
            pltpu.VMEM((8, 1024, 128), f32),
            pltpu.VMEM((8, 512, 128), f32),
            pltpu.VMEM((8, 512, 128), bf16),
            pltpu.VMEM((8, 480, 128), bf16),
            pltpu.VMEM((8, 64, 128), f32),
            pltpu.VMEM((8, 32, 128), f32),
            pltpu.VMEM((8, 1, 128), jnp.int32),
            pltpu.VMEM((8, 256, 512), bf16),
            pltpu.VMEM((32, 8, 128), f32),
            pltpu.VMEM((32, 8, 128), bf16),
            pltpu.VMEM((32, 8, 128), bf16),
            dma((2,)),
            dma((56,)),
            dma((64,)),
            dma((8,)),
            dma((8,)),
            dma((8,)),
            dma((8,)),
            dma((8,)),
            dma((8,)),
            dma((8,)),
            dma((8,)),
            dma((1,)),
            dma((1,)),
        ],
        compiler_params=pltpu.CompilerParams(
            collective_id=0, has_side_effects=True, vmem_limit_bytes=48 * 2**20
        ),
        name="influence",
    )(
        *(
            pltpu.with_memory_space_constraint(x, pltpu.HBM)
            for x in (
                query_grads, query_ids.reshape(1, 128), train_feats, basis_out[0], basis_in[0], eigen_vals[0]
            )
        )
    ) * (1.0 / math.sqrt(131072))


def solution(mesh):
    return jax.shard_map(
        on_device,
        mesh=mesh,
        in_specs=(
            P("group", "layer"),
            P("group"),
            P("group", "layer"),
            P("layer", None, None),
            P("layer", None, None),
            P("layer", None, None),
        ),
        out_specs=P("layer", "group"),
        check_vma=False,
    )
```

```python
import functools
import math

import jax
import jax.numpy as jnp
from jax import lax
from jax.experimental import pallas as pl
from jax.experimental.pallas import tpu as pltpu
from jax.sharding import PartitionSpec as P

damping = 0.1
MESH = pl.DeviceIdType.MESH
f32, bf16 = jnp.float32, jnp.bfloat16

ORDER = (
    ("a0", 512), ("b0", 384), ("b2", 384), ("a1", 640), ("a2", 512), ("b1", 512), ("b3", 512), ("a3", 640),
)
PIECES = {}
row = 0
for name, size in ORDER:
    PIECES[name] = (row, row + size)
    row += size
NAMES = list(PIECES)
A = ((0, 512), (1280, 2432), (3456, 4096))
B = ((512, 1280), (2432, 3456))
UP = ("0", "1", "2", "3")
LAST = 6
PITCH = 72
DOWN = ("2", "3", "0", "1")


def split(x):
    high = x.astype(bf16)
    return high, (x - high.astype(f32)).astype(bf16)


def diagonal(block):
    width = block.shape[0]
    four = jnp.concatenate([block] * 4, axis=1)
    four = jnp.concatenate([four] * 4, axis=0)
    rows = lax.broadcasted_iota(jnp.int32, four.shape, 0) // width
    cols = lax.broadcasted_iota(jnp.int32, four.shape, 1) // width
    return jnp.where(rows == cols, four, 0.0)


def far(n, count):
    return count // 2 + (n % 2 * 2 - 1) * ((n + 1) // 2)


def apply_basis(matrix, x):
    high, low = split(x)
    both = jnp.dot(matrix, high, preferred_element_type=f32)
    rest = jnp.dot(matrix[:256], low, preferred_element_type=f32)
    return both[:256] + both[256:] + rest


def kernel(
    g_hbm, ids_ref, t_hbm, bo_ref, bi_ref, eig_ref, out_ref,
    g_v, t_v, q, y1, y2, inv, bdm, acc, cx, rs_send, rs_recv, zs, xs, ids, hot, a_send, a_round, a_recv,
    load_sem, q_send, q_recv, id_send, id_recv, cx_ssem, cx_rsem, rs_ssem, rs_rsem, xs_ssem, xs_rsem, a_ssem, a_rsem,
):
    group, layer = lax.axis_index("group"), lax.axis_index("layer")
    xh, y = group // 4, group % 4
    me, core = layer // 2, layer % 2
    z, xl = me // 2, me % 2
    up = (xh * 4 + lax.rem(y + 1, 4), layer)
    down = (xh * 4 + lax.rem(y + 3, 4), layer)
    across = ((1 - xh) * 4 + y, layer)
    sibling = (group, me * 2 + 1 - core)

    load_g = pltpu.make_async_copy(g_hbm, g_v, load_sem.at[0])
    load_t = pltpu.make_async_copy(t_hbm, t_v, load_sem.at[1])
    load_g.start()

    barrier = pltpu.get_barrier_semaphore()

    def greet_group(k, c):
        pl.semaphore_signal(barrier, inc=1, device_id=(lax.rem(group + k, 8), layer), device_id_type=MESH)
        return c

    def greet_layer(n, c):
        to = lax.rem(layer + far(n, 32), 32)
        pl.semaphore_signal(barrier, inc=1, device_id=(group, to), device_id_type=MESH)
        return c

    lax.fori_loop(0, 31, greet_layer, 0, unroll=31)
    lax.fori_loop(1, 8, greet_group, 0, unroll=7)
    load_t.start()

    bo = diagonal(bo_ref[...])
    bi = diagonal(bi_ref[...])
    for place, matrix in enumerate((bi.T, bo.T, bo, bi)):
        high, low = split(matrix)
        bdm[place, 0:256, :] = high
        bdm[place, 256:512, :] = low
    scale = 1.0 / (eig_ref[...] + damping)
    for j in range(64):
        inv[j * 64 : j * 64 + 64, :] = jnp.broadcast_to(scale[:, j : j + 1], (64, 128))

    load_g.wait()

    def spread(ref, u, r):
        for h in range(2):
            for s in range(4):
                start = pl.multiple_of((u * 8 + h * 4 + s) * PITCH, 8)
                ref[pl.ds(start, 64), :] = r[s * 64 : s * 64 + 64, h * 128 : h * 128 + 128]

    def stage_a(u, c):
        base = pl.multiple_of(u * 512, 512)
        left = g_v[:, pl.ds(base, 256)]
        right = g_v[:, pl.ds(base + 256, 256)]
        both = lax.dot_general(
            bdm[0], jnp.concatenate([left, right], axis=0), (((1,), (1,)), ((), ())), preferred_element_type=f32
        )
        r = both[:256] + both[256:]
        spread(y1, u, r)
        return c

    def strided(ref, u):
        halves = []
        for h in range(2):
            halves.append(
                jnp.concatenate([ref[pl.ds(u * 8 + h * 4 + s, 64, stride=PITCH), :] for s in range(4)], axis=0)
            )
        return jnp.concatenate(halves, axis=1)

    def stage_bc(u, c):
        base = pl.multiple_of(u * 512, 512)
        r = apply_basis(bdm[1], strided(y1, u))
        r = r * jnp.concatenate([inv[pl.ds(base, 256), :], inv[pl.ds(base + 256, 256), :]], axis=1)
        r = apply_basis(bdm[2], r)
        spread(y2, u, r)
        return c

    def stage_d(u, c):
        base = pl.multiple_of(u * 512, 512)
        r = apply_basis(bdm[3], strided(y2, u)).astype(bf16)
        q[0, pl.ds(base, 256), :] = r[:, :128]
        q[0, pl.ds(base + 256, 256), :] = r[:, 128:]
        return c

    lax.fori_loop(0, 8, stage_a, 0, unroll=8)
    lax.fori_loop(0, 8, stage_bc, 0, unroll=8)
    lax.fori_loop(0, 3, stage_d, 0, unroll=3)

    pl.semaphore_wait(barrier, 38)

    sends = []

    def send(src_slot, piece, target, dst_slot):
        lo, hi = PIECES[piece]
        copy = pltpu.make_async_remote_copy(
            src_ref=q.at[src_slot, pl.ds(lo, hi - lo)],
            dst_ref=q.at[dst_slot, pl.ds(lo, hi - lo)],
            send_sem=q_send.at[len(sends)],
            recv_sem=q_recv.at[dst_slot * 8 + NAMES.index(piece)],
            device_id=target,
            device_id_type=MESH,
        )
        copy.start()
        sends.append(copy)

    def arrive(slot, piece):
        lo, hi = PIECES[piece]
        part = q.at[slot, pl.ds(lo, hi - lo)]
        pltpu.make_async_remote_copy(
            src_ref=part, dst_ref=part, send_sem=q_send.at[0], recv_sem=q_recv.at[slot * 8 + NAMES.index(piece)],
            device_id=up, device_id_type=MESH,
        ).wait_recv()

    send(0, "a0", across, 4)
    send(0, "b0", up, 3)
    send(0, "b2", down, 1)
    lax.fori_loop(3, 8, stage_d, 0, unroll=5)
    for n in "123":
        send(0, "a" + n, across, 4)
    for above, below in zip(UP[1:], DOWN[1:]):
        send(0, "b" + above, up, 3)
        send(0, "b" + below, down, 1)
    for n in "0123":
        send(0, "b" + n, across, 4)

    def id_target(k):
        return (lax.rem(xh + k // 4, 2) * 4 + lax.rem(y + k, 4), layer)

    def id_slot(k):
        return k // 4 * 4 + (4 - k % 4) % 4

    id_copies = []
    for k in range(1, 8):
        copy = pltpu.make_async_remote_copy(
            src_ref=ids_ref, dst_ref=ids.at[id_slot(k)], send_sem=id_send.at[id_slot(k)], recv_sem=id_recv.at[id_slot(k)],
            device_id=id_target(k), device_id_type=MESH,
        )
        copy.start()
        id_copies.append(copy)
    ids[0] = ids_ref[...]

    mine = pl.multiple_of(core * 512, 512)
    theirs = pl.multiple_of((1 - core) * 512, 512)

    def half(slot, ranges, first, start):
        r = None if first else acc[slot, pl.ds(start, 512), :]
        for lo, hi in ranges:
            term = jnp.dot(t_v[pl.ds(start, 512), lo:hi], q[slot, lo:hi, :], preferred_element_type=f32)
            r = term if r is None else r + term
        acc[slot, pl.ds(start, 512), :] = r

    def multiply(slot, ranges, first):
        def tile(i, c):
            half(slot, ranges, first, pl.multiple_of(i * 512, 512))
            return c

        lax.fori_loop(0, 2, tile, 0)

    def exchange(slot):
        return pltpu.make_async_remote_copy(
            src_ref=acc.at[slot, pl.ds(theirs, 512)], dst_ref=cx.at[slot], send_sem=cx_ssem.at[slot],
            recv_sem=cx_rsem.at[slot], device_id=sibling, device_id_type=MESH,
        )

    def scatter(slot):
        exchange(slot).wait_recv()
        rs_send[slot] = (acc[slot, pl.ds(mine, 512), :] + cx[slot]).astype(bf16)
        count, size = (16, 32) if slot == LAST else (8, 64)
        here = me if slot == LAST else z

        def one(n, c):
            k = far(n, count)
            to = lax.rem(here + k, count)
            target = to * 2 + core if slot == LAST else to * 4 + xl * 2 + core
            pltpu.make_async_remote_copy(
                src_ref=rs_send.at[slot, pl.ds(pl.multiple_of(to * size, size), size)],
                dst_ref=rs_recv.at[slot, pl.ds(pl.multiple_of((k - 1) * size, size), size)],
                send_sem=rs_ssem.at[slot], recv_sem=rs_rsem.at[slot],
                device_id=(group, target), device_id_type=MESH,
            ).start()
            return c

        lax.fori_loop(0, count - 1, one, 0, unroll=count - 1)

    def scattered(slot):
        landed = rs_recv.at[slot, pl.ds(0, 480 if slot == LAST else 448)]
        return pltpu.make_async_remote_copy(
            src_ref=landed, dst_ref=landed, send_sem=rs_ssem.at[slot], recv_sem=rs_rsem.at[slot],
            device_id=up, device_id_type=MESH,
        )

    def summed(slot, size):
        scattered(slot).wait_recv()
        own = pl.multiple_of((me if slot == LAST else z) * size, size)
        total = acc[slot, pl.ds(mine + own, size), :] + cx[slot, pl.ds(own, size), :]
        for k in range(512 // size - 1):
            total = total + rs_recv[slot, k * size : k * size + size, :].astype(f32)
        return total

    def swap(slot):
        return pltpu.make_async_remote_copy(
            src_ref=zs.at[slot, pl.ds(pl.multiple_of((1 - xl) * 32, 32), 32)], dst_ref=xs.at[slot],
            send_sem=xs_ssem.at[slot], recv_sem=xs_rsem.at[slot],
            device_id=(group, z * 4 + (1 - xl) * 2 + core), device_id_type=MESH,
        )

    def zsum(slot):
        zs[slot] = summed(slot, 64)

    def collect(slot):
        if slot == LAST:
            total = summed(slot, 32)
        else:
            swap(slot).wait_recv()
            total = zs[slot, pl.ds(pl.multiple_of(xl * 32, 32), 32), :] + xs[slot]
        spread = []
        for half_total in split(total):
            none = jnp.zeros_like(half_total)
            spread.append(
                jnp.concatenate(
                    [jnp.concatenate([half_total if m == k else none for m in range(4)], axis=1) for k in range(4)],
                    axis=0,
                )
            )
        placed = lax.dot_general(
            jnp.concatenate([hot[slot], hot[slot]], axis=1), jnp.concatenate(spread, axis=1),
            (((1,), (1,)), ((), ())), preferred_element_type=f32,
        )
        placed = placed.reshape(32, 8, 128)
        a_send[...] = placed if slot == 0 else a_send[...] + placed

    def piece(slot, name, first):
        arrive(slot, name)
        multiply(slot, (PIECES[name],), first)

    load_t.wait()
    multiply(0, ((0, 4096),), True)
    exchange(0).start()

    def neighbours_b(above, below):
        arrive(3, "b" + above)
        arrive(1, "b" + below)
        if above in "01":
            send(3, "b" + above, up, 2)
            send(1, "b" + below, down, 2)
        send(3, "b" + above, across, 7)
        send(1, "b" + below, across, 5)

    def partner_a(n):
        arrive(4, "a" + n)
        send(4, "a" + n, up, 7)
        send(4, "a" + n, down, 5)

    def neighbours_a(above, below):
        arrive(3, "a" + above)
        arrive(1, "a" + below)
        if above in "01":
            send(3, "a" + above, up, 2)
            send(1, "a" + below, down, 2)

    def second_a(above, below):
        arrive(7, "a" + above)
        arrive(5, "a" + below)
        if above in "01":
            send(7, "a" + above, up, 6)
            send(5, "a" + below, down, 6)

    neighbours_b("0", "2")
    neighbours_b("1", "3")
    for above, below in zip(UP, DOWN):
        send(0, "a" + above, up, 3)
        send(0, "a" + below, down, 1)
    partner_a("0")
    scatter(0)
    partner_a("1")
    neighbours_b("2", "0")
    neighbours_b("3", "1")
    partner_a("2")

    for copy in id_copies:
        copy.wait_recv()
    rows = lax.broadcasted_iota(jnp.int32, (256, 128), 0)
    rows = rows // 8 * 32 + rows % 8
    for s in range(8):
        for k in range(4):
            same = rows + 8 * k == ids[s]
            hot[s, :, k * 128 : k * 128 + 128] = jnp.where(same, 1.0, 0.0).astype(bf16)

    partner_a("3")
    multiply(4, A, True)
    for n in "0213":
        arrive(2, "b" + n)
        send(2, "b" + n, across, 6)
    multiply(3, B, True)
    multiply(1, B, True)
    neighbours_a("0", "2")
    multiply(2, B, True)
    neighbours_a("1", "3")
    for n in "0123":
        arrive(4, "b" + n)
    multiply(4, B, False)
    exchange(4).start()
    zsum(0)
    neighbours_a("2", "0")
    scatter(4)
    neighbours_a("3", "1")
    multiply(3, A, False)
    exchange(3).start()
    multiply(1, A, False)
    exchange(1).start()
    second_a("0", "2")
    scatter(3)
    second_a("1", "3")
    scatter(1)
    zsum(4)
    second_a("2", "0")
    second_a("3", "1")
    multiply(7, A, True)
    multiply(5, A, True)
    zsum(3)
    for n in "0123":
        arrive(7, "b" + n)
    multiply(7, B, False)
    exchange(7).start()
    for n in "0123":
        arrive(5, "b" + n)
    multiply(5, B, False)
    exchange(5).start()
    zsum(1)
    for n in "0213":
        arrive(2, "a" + n)
    scatter(7)
    multiply(2, A, False)
    exchange(2).start()
    scatter(5)
    for slot in (0, 4, 3, 1):
        swap(slot).start()
    piece(6, "b0", True)
    piece(6, "b2", False)
    scatter(2)
    piece(6, "a0", False)
    piece(6, "a2", False)
    piece(6, "b1", False)
    piece(6, "b3", False)
    arrive(6, "a1")
    arrive(6, "a3")
    half(6, (PIECES["a1"], PIECES["a3"]), False, theirs)
    exchange(6).start()
    half(6, (PIECES["a1"], PIECES["a3"]), False, mine)
    collect(0)
    collect(4)
    scatter(6)
    for slot in (7, 5, 2):
        zsum(slot)
        swap(slot).start()
    collect(3)
    collect(1)
    collect(7)
    collect(5)
    collect(2)
    collect(6)

    place = core * 16 + me
    a_round[...] = a_send[...].astype(bf16)

    def deal(n, c):
        to = lax.rem(layer + far(n, 32), 32)
        pltpu.make_async_remote_copy(
            src_ref=a_round.at[to], dst_ref=a_recv.at[place], send_sem=a_ssem.at[0], recv_sem=a_rsem.at[0],
            device_id=(group, to), device_id_type=MESH,
        ).start()
        return c

    lax.fori_loop(0, 31, deal, 0, unroll=31)
    a_recv[place] = a_round[layer]
    dealt = pltpu.make_async_remote_copy(
        src_ref=a_recv.at[pl.ds(0, 31)], dst_ref=a_recv.at[pl.ds(0, 31)], send_sem=a_ssem.at[0], recv_sem=a_rsem.at[0],
        device_id=up, device_id_type=MESH,
    )
    for copy in sends:
        copy.wait_send()
    for copy in id_copies:
        copy.wait_send()
    for slot in range(8):
        exchange(slot).wait_send()
        scattered(slot).wait_send()
        if slot != LAST:
            swap(slot).wait_send()
    dealt.wait_recv()
    for m in range(8):
        tiles = [a_recv[4 * m + n].astype(f32) for n in range(4)]
        for k in range(4):
            out_ref[8 * k : 8 * k + 8, 128 * m : 128 * m + 128] = jnp.concatenate(
                [tile[:, 32 * k : 32 * k + 32] for tile in tiles], axis=1
            )

    dealt.wait_send()


def on_device(query_grads, query_ids, train_feats, basis_out, basis_in, eigen_vals):
    anywhere = pl.BlockSpec(memory_space=pl.ANY)
    vmem = pl.BlockSpec(memory_space=pltpu.VMEM)
    dma = pltpu.SemaphoreType.DMA
    return pl.pallas_call(
        kernel,
        out_shape=jax.ShapeDtypeStruct((32, 1024), f32),
        in_specs=[anywhere, vmem, anywhere, vmem, vmem, vmem],
        out_specs=vmem,
        scratch_shapes=[
            pltpu.VMEM((128, 4096), bf16),
            pltpu.VMEM((1024, 4096), bf16),
            pltpu.VMEM((8, 4096, 128), bf16),
            pltpu.VMEM((65 * PITCH, 128), f32),
            pltpu.VMEM((65 * PITCH, 128), f32),
            pltpu.VMEM((4096, 128), f32),
            pltpu.VMEM((4, 512, 256), bf16),
            pltpu.VMEM((8, 1024, 128), f32),
            pltpu.VMEM((8, 512, 128), f32),
            pltpu.VMEM((8, 512, 128), bf16),
            pltpu.VMEM((8, 480, 128), bf16),
            pltpu.VMEM((8, 64, 128), f32),
            pltpu.VMEM((8, 32, 128), f32),
            pltpu.VMEM((8, 1, 128), jnp.int32),
            pltpu.VMEM((8, 256, 512), bf16),
            pltpu.VMEM((32, 8, 128), f32),
            pltpu.VMEM((32, 8, 128), bf16),
            pltpu.VMEM((32, 8, 128), bf16),
            dma((2,)),
            dma((56,)),
            dma((64,)),
            dma((8,)),
            dma((8,)),
            dma((8,)),
            dma((8,)),
            dma((8,)),
            dma((8,)),
            dma((8,)),
            dma((8,)),
            dma((1,)),
            dma((1,)),
        ],
        compiler_params=pltpu.CompilerParams(
            collective_id=0, has_side_effects=True, vmem_limit_bytes=48 * 2**20
        ),
        name="influence",
    )(
        *(
            pltpu.with_memory_space_constraint(x, pltpu.HBM)
            for x in (
                query_grads, query_ids.reshape(1, 128), train_feats, basis_out[0], basis_in[0], eigen_vals[0]
            )
        )
    ) * (1.0 / math.sqrt(131072))


def solution(mesh):
    return jax.shard_map(
        on_device,
        mesh=mesh,
        in_specs=(
            P("group", "layer"),
            P("group"),
            P("group", "layer"),
            P("layer", None, None),
            P("layer", None, None),
            P("layer", None, None),
        ),
        out_specs=P("layer", "group"),
        check_vma=False,
    )
```
